32 devices in a mesh: bins: 8 (over z, x), xy: 4 (over y, core).
Axes of the slice: x: 2, y: 2, z: 4, core: 2. Of those that a mesh axis runs over, the one named last changes fastest.
Arguments:
- conc: float32 [8, 128, 16, 256], P('bins', None, 'xy'), may hold values from 0.05 to 2
- vel_x: float32 [8, 16, 256], P('bins', 'xy'), may hold values from -0.3 to 0.3
- vel_y: float32 [8, 16, 256], P('bins', 'xy'), may hold values from -0.3 to 0.3
- sea_mask: int32 [16, 256], P('xy'), may hold values 0 or 1
- settle: float32 [128], replicated, may hold values from 0.05 to 0.6
- size_bin_kernel_class: int32 [128], replicated, may hold values from 0 to 7
- aggregate_upward_factor: float32 [8], replicated, may hold values from 0.25 to 2
- agg_down: float32 [8], replicated, may hold values from 0.25 to 2
- break_rate: float32 [8], replicated, may hold values from 0.05 to 0.5
Outputs:
- conc_next: float32 [8, 128, 16, 256], P('bins', None, 'xy')
The draws below stay inside these ranges and needn't reach their ends.
All inputs are finite; a program needn't handle non-finite values. No bound on the sum of `sea_mask` on one device may be relied on, other than what follows from the above.
Results may differ from the reference program's by a relative error of at most 0.00007.
Values sent between devices are 32-bit elements; how exact they have to be, the bound alone decides.
No kernel may reach another device: no remote copies, remote signals or barrier semaphores. Data moves between devices by JAX's collectives and lax.ppermute only.
A program may use at most 64 MiB of HBM per device.

```python
import math
import jax
import jax.numpy as jnp
from jax import lax

NB = 128
NCLS = 8
GY = 256
HSUB = 2
VERTICAL_SUBSTEP = 2
LEV = 8
GX = 16


def with_ends(array, own_key, low, top_value):
    place = [jax.random.randint(jax.random.fold_in(own_key, axis), (), 0, length) for axis, length in enumerate(array.shape)]
    longest = array.shape.index(max(array.shape))
    neighbour = place[:longest] + [(place[longest] + 1) % array.shape[longest]] + place[longest + 1:]
    return array.at[tuple(place)].set(low).at[tuple(neighbour)].set(top_value)


def levels(own_key, shape, cuts, smallest, largest):
    def one(dim, parts):
        heights = jax.random.uniform(jax.random.fold_in(jax.random.fold_in(own_key, 6), dim), (parts,), jnp.float32, smallest / len(cuts), largest / len(cuts))
        return jnp.repeat(jnp.exp(heights), shape[dim] // parts).reshape((-1,) + (1,) * (len(shape) - dim - 1))

    level = one(*cuts[0])
    for cut in cuts[1:]:
        level = level * one(*cut)
    return level


def setup_inputs(seed: int = 0) -> dict:
    splits = jax.random.split(jax.random.key(seed), 10)
    conc = jnp.clip(jnp.exp(math.log(2.0) - 3.6888794 * jax.random.uniform(splits[0], (LEV, NB, GX, GY), jnp.float32) ** levels(splits[0], (LEV, NB, GX, GY), ((0, 8), (2, 4)), -0.2, 0.2)), 0.05, 2.0)
    vel_x = jnp.clip(jax.random.uniform(splits[1], (LEV, GX, GY), jnp.float32, -0.3, 0.3) * levels(splits[1], (LEV, GX, GY), ((0, 8), (1, 4)), -0.4, 0.0), -0.3, 0.3)
    vel_y = jnp.clip(jax.random.uniform(splits[2], (LEV, GX, GY), jnp.float32, -0.3, 0.3) * levels(splits[2], (LEV, GX, GY), ((0, 8), (1, 4)), -0.4, 0.0), -0.3, 0.3)
    sea_mask = with_ends((jax.random.randint(splits[3], (GX, GY), 0, 4) < 3).astype(jnp.int32), jax.random.fold_in(splits[3], 1), 0, 1)
    settle = jnp.clip(jnp.exp(jax.random.uniform(splits[4], (NB,), jnp.float32, math.log(0.05), math.log(0.6))), 0.05, 0.6)
    size_bin_kernel_class = with_ends(jax.random.randint(splits[5], (NB,), 0, NCLS), jax.random.fold_in(splits[5], 1), 0, NCLS - 1).astype(jnp.int32)
    aggregate_upward_factor = jnp.clip(jnp.exp(jax.random.uniform(splits[6], (NCLS,), jnp.float32, math.log(0.25), math.log(2.0))), 0.25, 2.0)
    agg_down = jnp.clip(jnp.exp(jax.random.uniform(splits[7], (NCLS,), jnp.float32, math.log(0.25), math.log(2.0))), 0.25, 2.0)
    break_rate = jnp.clip(jnp.exp(jax.random.uniform(splits[8], (NCLS,), jnp.float32, math.log(0.05), math.log(0.5))), 0.05, 0.5)
    return {"conc": conc, "vel_x": vel_x, "vel_y": vel_y, "sea_mask": sea_mask, "settle": settle, "size_bin_kernel_class": size_bin_kernel_class, "aggregate_upward_factor": aggregate_upward_factor, "agg_down": agg_down, "break_rate": break_rate}


h_diffusion = 0.2
v_diffusion = 0.2
step_duration = 0.5
collide_scale = 2.0


def settle_mix(column, sink):
    flux = sink * column
    above = jnp.concatenate([jnp.zeros_like(flux[:1]), flux[:-1]], 0)
    upper = jnp.concatenate([column[:1], column[:-1]], 0)
    lower = jnp.concatenate([column[1:], column[-1:]], 0)
    return column - flux + above + v_diffusion * (upper + lower - 2.0 * column)


def reference(conc, vel_x, vel_y, sea_mask, settle, size_bin_kernel_class, aggregate_upward_factor, agg_down, break_rate):
    water = sea_mask.astype(jnp.float32)

    def horizontal(packed):
        level, speed_x, speed_y = packed
        for unused_item in range(HSUB):
            padded = jnp.pad(level, ((0, 0), (1, 1), (1, 1)))
            east = padded[:, 2:, 1:-1]
            west = padded[:, :-2, 1:-1]
            north = padded[:, 1:-1, 2:]
            south = padded[:, 1:-1, :-2]
            level = water * (level - 0.5 * speed_x * (east - west) - 0.5 * speed_y * (north - south)
                             + h_diffusion * (east + west + north + south - 4.0 * level))
        return level

    moved = lax.map(horizontal, (conc, vel_x, vel_y))
    sink = settle[:, None]
    up_rate = aggregate_upward_factor[size_bin_kernel_class][:, None]
    down_rate = agg_down[size_bin_kernel_class][:, None]
    brk_rate = break_rate[size_bin_kernel_class][:, None]
    bin_index = jnp.arange(NB)
    weight = (1.0 / jnp.maximum(bin_index, 1).astype(jnp.float32))[:, None]
    broken = (bin_index >= 1).astype(jnp.float32)[:, None]

    def column_row(block):
        for unused_item in range(VERTICAL_SUBSTEP):
            block = settle_mix(block, sink)
        up_terms = up_rate * block
        lower_sum = jnp.cumsum(up_terms, 1) - up_terms
        down_terms = down_rate * block
        higher_sum = jnp.sum(down_terms, 1, keepdims=True) - jnp.cumsum(down_terms, 1)
        fragmentation_terms = brk_rate * block * weight
        frag_sum = jnp.sum(fragmentation_terms, 1, keepdims=True) - jnp.cumsum(fragmentation_terms, 1)
        concentration_change = (collide_scale / NB) * (down_rate * block * lower_sum - up_rate * block * higher_sum)
        return block + step_duration * (concentration_change + frag_sum - brk_rate * broken * block)

    rows = jnp.moveaxis(moved, 2, 0)
    result = lax.map(column_row, rows)
    return jnp.moveaxis(result, 0, 2)
```

```python
import jax
import jax.numpy as jnp
from jax import lax
from jax.sharding import PartitionSpec as P

NB = 128
NCLS = 8

h_diffusion = 0.2
v_diffusion = 0.2
step_duration = 0.5
collide_scale = 2.0


def swap(value, axis, reach, parity):
    count = lax.axis_size(axis)
    pairs = []
    for low in range(count - reach):
        if (low // reach) % 2 == parity:
            pairs += [(low, low + reach), (low + reach, low)]
    return lax.ppermute(value, axis, pairs)


def substep(padded, speed_x, speed_y, water):
    level = padded[1:-1]
    east = padded[2:]
    west = padded[:-2]
    side = jnp.pad(level, ((0, 0), (0, 0), (1, 1)))
    north = side[:, :, 2:]
    south = side[:, :, :-2]
    return water * (
        level
        - 0.5 * speed_x * (east - west)
        - 0.5 * speed_y * (north - south)
        + h_diffusion * (east + west + north + south - 4.0 * level)
    )


def horizontal(rows, speed_x, speed_y, water):
    count, bins, cols = rows.shape
    odd = lax.axis_index("xy") % 2 == 1

    def message(low, high):
        edge = rows[:2] if low else rows[count - 2 :]
        at = 0 if low else count - 1
        aux = jnp.stack([speed_x[at], speed_y[at], water[at]])
        return jnp.concatenate([edge.reshape(2 * bins, cols), jnp.pad(aux, ((0, 5), (0, 0)))], 0)

    low, high = message(True, False), message(False, True)
    got_a = swap(jnp.where(odd, low, high), "xy", 1, 0)
    got_b = swap(jnp.where(odd, high, low), "xy", 1, 1)
    above = jnp.where(odd, got_a, got_b)
    below = jnp.where(odd, got_b, got_a)

    def split(got):
        return got[: 2 * bins].reshape(2, bins, cols), got[2 * bins : 2 * bins + 3]

    top, top_aux = split(above)
    bottom, bottom_aux = split(below)
    ext = jnp.concatenate([top, rows, bottom], 0)
    aux = [
        jnp.concatenate([top_aux[i : i + 1], own, bottom_aux[i : i + 1]], 0)[:, None]
        for i, own in enumerate((speed_x, speed_y, water))
    ]
    once = substep(ext, *aux)
    return substep(once, *[part[1:-1] for part in aux])


def local(
    conc,
    vel_x,
    vel_y,
    sea_mask,
    settle,
    size_bin_kernel_class,
    aggregate_upward_factor,
    agg_down,
    break_rate,
):
    rows = jnp.transpose(conc[0], (1, 0, 2))
    water = sea_mask.astype(jnp.float32)
    moved = horizontal(rows, vel_x[0], vel_y[0], water)

    levels = lax.axis_size("bins")
    k = lax.axis_index("bins")
    odd = k % 2 == 1
    high_z = (k // 2) % 2 == 1
    fall = settle + v_diffusion
    rise = v_diffusion

    def keep(level):
        inner = (level > 0).astype(jnp.float32) + (level < levels - 1).astype(jnp.float32)
        return 1.0 - settle - v_diffusion * inner

    inner = (k > 0).astype(jnp.float32) + (k < levels - 1).astype(jnp.float32)
    on_self = keep(k) * keep(k) + inner * fall * rise
    on_up2 = fall * fall
    on_down2 = jnp.full_like(settle, rise * rise)
    on_up1 = fall * (keep(k + 1) + keep(k))
    on_down1 = rise * (keep(k - 1) + keep(k))

    def col(vector):
        return vector[None, :, None]

    half = NB // 2
    c_a, c_b = moved[:, :half], moved[:, half:]

    a0 = swap(c_a, "bins", 2, 0)
    a1 = swap(c_a, "bins", 2, 1)
    b_pair = swap(c_b, "bins", 1, 0)

    pair_own = jnp.where(odd, on_down1, on_up1)
    pair_far = jnp.where(odd, fall * (keep(k - 1) + keep(k - 2)), rise * (keep(k + 1) + keep(k + 2)))
    zero = jnp.zeros_like(settle)
    in_first = odd == high_z
    pair_0 = jnp.where(in_first, pair_far, zero)
    pair_1 = jnp.where(in_first, zero, pair_far)
    send_pair = (
        col(pair_own[:half]) * c_a + col(pair_0[:half]) * a0 + col(pair_1[:half]) * a1
    )
    up_pair = jnp.where(odd, zero, fall * (keep(k + 2) + keep(k + 1)))
    down_pair = jnp.where(odd, rise * (keep(k - 2) + keep(k - 1)), zero)
    send0 = col(jnp.where(high_z, on_down2, on_up2)[half:]) * c_b + col(jnp.where(high_z, down_pair, up_pair)[half:]) * b_pair
    send1 = col(jnp.where(high_z, on_up2, on_down2)[half:]) * c_b + col(jnp.where(high_z, up_pair, down_pair)[half:]) * b_pair

    b0 = swap(send0, "bins", 2, 0)
    b1 = swap(send1, "bins", 2, 1)
    a_pair = swap(send_pair, "bins", 1, 0)

    far_0 = jnp.where(high_z, on_up2, on_down2)
    far_1 = jnp.where(high_z, on_down2, on_up2)
    sunk_a = col(on_self[:half]) * c_a + col(far_0[:half]) * a0 + col(far_1[:half]) * a1 + a_pair
    from_pair = jnp.where(odd, fall * (keep(k) + keep(k - 1)), rise * (keep(k) + keep(k + 1)))
    sunk_b = col(on_self[half:]) * c_b + col(from_pair[half:]) * b_pair + b0 + b1
    sunk = jnp.concatenate([sunk_a, sunk_b], 1)

    onehot = (size_bin_kernel_class[:, None] == jnp.arange(NCLS)[None, :]).astype(jnp.float32)

    def lookup(table):
        return jnp.sum(onehot * table[None, :], 1)

    up_rate = lookup(aggregate_upward_factor)
    down_rate = lookup(agg_down)
    brk_rate = lookup(break_rate)
    index = jnp.arange(NB)
    i, j = index[None, :], index[:, None]
    weight = 1.0 / jnp.maximum(index, 1).astype(jnp.float32)
    pairs = jnp.where(i < j, down_rate[:, None] * up_rate[None, :], 0.0) - jnp.where(
        i > j, up_rate[:, None] * down_rate[None, :], 0.0
    )
    pieces = jnp.where(i > j, (brk_rate * weight)[None, :], 0.0) - jnp.where(
        (i == j) & (j >= 1), brk_rate[:, None], 0.0
    )
    both = jnp.concatenate([pairs * (step_duration * collide_scale / NB), pieces * step_duration], 0)
    sums = jnp.einsum("ji,ric->rjc", both, sunk, precision=lax.Precision.HIGHEST)
    result = sunk + sunk * sums[:, :NB] + sums[:, NB:]
    return jnp.transpose(result, (1, 0, 2))[None]


def solution(mesh):
    placed = (
        P("bins", None, "xy", None),
        P("bins", "xy", None),
        P("bins", "xy", None),
        P("xy", None),
        P(),
        P(),
        P(),
        P(),
        P(),
    )
    return jax.shard_map(
        local, mesh=mesh, in_specs=placed, out_specs=P("bins", None, "xy", None), check_vma=False
    )
```

```python
import functools

import jax
import jax.numpy as jnp
from jax import lax
from jax.experimental import pallas as pl
from jax.experimental.pallas import tpu as pltpu
from jax.sharding import PartitionSpec as P

NB = 128
NCLS = 8

h_diffusion = 0.2
v_diffusion = 0.2
step_duration = 0.5
collide_scale = 2.0
SUBLANES = 8
EDGE = 2
CHUNKS = ((0, 0, 128, True), (1, 0, 128, False))
VMEM = pl.BlockSpec(memory_space=pltpu.VMEM)
HBM = pl.BlockSpec(memory_space=pltpu.HBM)
PARAMS = pltpu.CompilerParams(vmem_limit_bytes=8 << 20)


def in_vmem(*values):
    return [pltpu.with_memory_space_constraint(value, pltpu.VMEM) for value in values]


def in_hbm(*values):
    return [pltpu.with_memory_space_constraint(value, pltpu.HBM) for value in values]


def odd_core():
    return lax.axis_index("xy") % 2 == 1


def by_parity(body):
    odd = odd_core()
    pl.when(odd)(functools.partial(body, True))
    pl.when(jnp.logical_not(odd))(functools.partial(body, False))


def swap(value, axis, reach, parity):
    count = lax.axis_size(axis)
    pairs = []
    for low in range(count - reach):
        if (low // reach) % 2 == parity:
            pairs += [(low, low + reach), (low + reach, low)]
    return lax.ppermute(value, axis, pairs)


def load_kernel(conc, vel_x, vel_y, mask, rows, near, far, flow, mask_rows, sems):
    count, bins, _ = rows.shape

    def body(odd):
        near_at, far_at = (0, count - EDGE) if odd else (count - EDGE, 0)
        copies = [pltpu.make_async_copy(mask, mask_rows, sems.at[0])]
        copies.append(pltpu.make_async_copy(vel_x.at[0], flow.at[0], sems.at[1]))
        copies.append(pltpu.make_async_copy(vel_y.at[0], flow.at[1], sems.at[2]))
        for target, at in ((near, near_at), (far, far_at)):
            for r in range(EDGE):
                copies.append(
                    pltpu.make_async_copy(
                        conc.at[0, :, at + r, :], target.at[r, pl.ds(0, bins)], sems.at[len(copies)]
                    )
                )
        for r in range(count):
            copies.append(pltpu.make_async_copy(conc.at[0, :, r, :], rows.at[r], sems.at[len(copies)]))
        for copy in copies:
            copy.start()
        for copy in copies[:3]:
            copy.wait()
        flow[2] = mask_rows[...].astype(jnp.float32)
        for target, end in ((near, 0 if odd else count - 1), (far, count - 1 if odd else 0)):
            for r in range(EDGE):
                target[r, bins:, :] = jnp.zeros_like(target[r, bins:, :])
            for i in range(3):
                target[0, bins + i : bins + i + 1, :] = flow[i, end : end + 1, :]
        for copy in copies[3:]:
            copy.wait()

    by_parity(body)


def load(conc, vel_x, vel_y, mask):
    _, bins, count, cols = conc.shape
    edge = pltpu.VMEM((EDGE, bins + SUBLANES, cols), jnp.float32)
    return pl.pallas_call(
        load_kernel,
        out_shape=(
            pltpu.VMEM((count, bins, cols), jnp.float32),
            edge,
            edge,
            pltpu.VMEM((3, count, cols), jnp.float32),
        ),
        in_specs=[HBM] * 4,
        out_specs=(VMEM,) * 4,
        scratch_shapes=[pltpu.VMEM((count, cols), jnp.int32), pltpu.SemaphoreType.DMA((3 + 2 * EDGE + count,))],
        compiler_params=PARAMS,
    )(*in_hbm(conc, vel_x, vel_y, mask))


def horizontal_kernel(near, rows_ref, halo_ref, flow_ref, out_ref, scale_ref):
    count, bins, cols = rows_ref.shape
    column = lax.broadcasted_iota(jnp.int32, (1, cols), 1)
    block = 4 * SUBLANES

    def body(odd):
        first = odd == near
        base = 0 if first else count - 4

        def row(i):
            if first:
                return (halo_ref, i) if i < EDGE else (rows_ref, i - EDGE)
            return (rows_ref, base + i) if i < 4 else (halo_ref, i - 4)

        for i in range(1, 5):
            ref, at = row(i)
            if ref is halo_ref:
                aux = halo_ref[0, bins : bins + SUBLANES, :]
                x, y, water = aux[0:1], aux[1:2], aux[2:3]
            else:
                x, y, water = (flow_ref[part, at : at + 1, :] for part in range(3))
            x, y = 0.5 * x, 0.5 * y
            parts = (
                water * (1.0 - 4.0 * h_diffusion),
                water * (h_diffusion - x),
                water * (h_diffusion + x),
                jnp.where(column == cols - 1, 0.0, water * (h_diffusion - y)),
                jnp.where(column == 0, 0.0, water * (h_diffusion + y)),
            )
            for number, part in enumerate(parts):
                scale_ref[i - 1, number] = jnp.broadcast_to(part, (SUBLANES, cols))

        def step(cells, i):
            own, east, west, north, south = (
                jnp.concatenate([scale_ref[i - 1, number]] * (block // SUBLANES), 0) for number in range(5)
            )
            here = cells[i]
            return (
                own * here
                + east * cells[i + 1]
                + west * cells[i - 1]
                + north * pltpu.roll(here, cols - 1, 1)
                + south * pltpu.roll(here, 1, 1)
            )

        for at in range(0, bins, block):
            at = pl.ds(at, block)
            cells = {}
            for i in range(6):
                ref, place = row(i)
                cells[i] = ref[place, at, :]
            once = {i: step(cells, i) for i in range(1, 5)}
            for i in range(EDGE):
                out_ref[i, at, :] = step(once, EDGE + i)

    by_parity(body)


def horizontal(near, rows, halo, flow):
    _, bins, cols = rows.shape
    return pl.pallas_call(
        functools.partial(horizontal_kernel, near),
        out_shape=pltpu.VMEM((EDGE, bins, cols), jnp.float32),
        in_specs=[VMEM] * 3,
        out_specs=VMEM,
        scratch_shapes=[pltpu.VMEM((4, 5, SUBLANES, cols), jnp.float32)],
        cost_estimate=pl.CostEstimate(flops=6 * 9 * bins * cols, bytes_accessed=32 * bins * cols, transcendentals=0),
        compiler_params=PARAMS,
    )(*in_vmem(rows, halo, flow))


def split(value):
    high = value.astype(jnp.bfloat16)
    return high, (value - high.astype(jnp.float32)).astype(jnp.bfloat16)


def collide_kernel(near, cells_ref, both_ref, *refs):
    out_ref, done_ref, sems = refs[-3:]
    count = out_ref.shape[2]

    def body(odd):
        at = 0 if odd == near else count - EDGE
        copies = []
        for r in range(EDGE):
            cells = cells_ref[r]
            high, low = split(cells)
            sums = jnp.dot(
                both_ref[...], jnp.concatenate([high, low, high], 0), preferred_element_type=jnp.float32
            )
            done_ref[r] = cells + cells * sums[:NB] + sums[NB:]
            copies.append(pltpu.make_async_copy(done_ref.at[r], out_ref.at[0, :, at + r, :], sems.at[r]))
            copies[-1].start()
        for copy in copies:
            copy.wait()

    by_parity(body)


def collide(near, cells, both, shape, before=None):
    rest = () if before is None else (before,)
    return pl.pallas_call(
        functools.partial(collide_kernel, near),
        out_shape=pltpu.HBM(shape, jnp.float32),
        in_specs=[VMEM] * 2 + [HBM] * len(rest),
        out_specs=HBM,
        input_output_aliases={2: 0} if rest else {},
        scratch_shapes=[pltpu.VMEM(cells.shape, jnp.float32), pltpu.SemaphoreType.DMA((EDGE,))],
        cost_estimate=pl.CostEstimate(flops=4 * 3 * NB * cells.size, bytes_accessed=12 * cells.size, transcendentals=0),
        compiler_params=PARAMS,
    )(*in_vmem(cells, both), *in_hbm(*rest))


def after(value, done):
    return lax.optimization_barrier((value, done))[0]


def local(
    conc,
    vel_x,
    vel_y,
    sea_mask,
    settle,
    size_bin_kernel_class,
    aggregate_upward_factor,
    agg_down,
    break_rate,
):
    rows, near_edge, far_edge, flow = load(conc, vel_x, vel_y, sea_mask)
    halo_core = swap(near_edge, "xy", 1, 0)
    halo_chip = swap(far_edge, "xy", 1, 1)
    near = horizontal(True, rows, halo_core, flow)
    halo_chip = after(halo_chip, near)
    settle, size_bin_kernel_class, aggregate_upward_factor, agg_down, break_rate, _ = lax.optimization_barrier(
        (settle, size_bin_kernel_class, aggregate_upward_factor, agg_down, break_rate, near)
    )
    moved = [near, horizontal(False, rows, halo_chip, flow)]

    levels = lax.axis_size("bins")
    k = lax.axis_index("bins")
    odd = k % 2 == 1
    high_z = (k // 2) % 2 == 1
    fall = settle + v_diffusion
    rise = jnp.full_like(settle, v_diffusion)

    def keep(level):
        inner = (level > 0).astype(jnp.float32) + (level < levels - 1).astype(jnp.float32)
        return 1.0 - settle - v_diffusion * inner

    inner = (k > 0).astype(jnp.float32) + (k < levels - 1).astype(jnp.float32)
    on_self = keep(k) * keep(k) + inner * fall * rise
    up2, down2 = fall * fall, rise * rise
    zero = jnp.zeros_like(settle)
    up_pair = jnp.where(odd, zero, fall * (keep(k + 2) + keep(k + 1)))
    down_pair = jnp.where(odd, rise * (keep(k - 2) + keep(k - 1)), zero)
    send_0 = (jnp.where(high_z, down2, up2), jnp.where(high_z, down_pair, up_pair))
    send_1 = (jnp.where(high_z, up2, down2), jnp.where(high_z, up_pair, down_pair))
    from_pair = jnp.where(odd, fall * (keep(k) + keep(k - 1)), rise * (keep(k) + keep(k + 1)))
    pair_own = jnp.where(odd, rise * (keep(k - 1) + keep(k)), fall * (keep(k + 1) + keep(k)))
    pair_far = jnp.where(odd, fall * (keep(k - 1) + keep(k - 2)), rise * (keep(k + 1) + keep(k + 2)))
    far_0 = jnp.where(high_z, up2, down2)
    far_1 = jnp.where(high_z, down2, up2)
    uses_0 = odd == high_z

    def total(low, high, *terms):
        out = None
        for scale, cells in terms:
            part = cells if scale is None else scale[low:high][None, :, None] * cells
            out = part if out is None else out + part
        return out

    onehot = (size_bin_kernel_class[:, None] == jnp.arange(NCLS)[None, :]).astype(jnp.float32)

    def lookup(table):
        return jnp.sum(onehot * table[None, :], 1)

    up_rate = lookup(aggregate_upward_factor)
    down_rate = lookup(agg_down)
    brk_rate = lookup(break_rate)
    index = jnp.arange(NB)
    i, j = index[None, :], index[:, None]
    weight = 1.0 / jnp.maximum(index, 1).astype(jnp.float32)
    pairs = jnp.where(i < j, down_rate[:, None] * up_rate[None, :], 0.0) - jnp.where(
        i > j, up_rate[:, None] * down_rate[None, :], 0.0
    )
    pieces = jnp.where(i > j, (brk_rate * weight)[None, :], 0.0) - jnp.where(
        (i == j) & (j >= 1), brk_rate[:, None], 0.0
    )
    both = jnp.concatenate([pairs * (step_duration * collide_scale / NB), pieces * step_duration], 0)

    high = lax.reduce_precision(both, 8, 7)
    low = both - high
    both = jnp.concatenate([high, high, low], 1).astype(jnp.bfloat16)

    first = []
    for far, low, high, x_first in CHUNKS:
        cells = moved[far][:, low:high]
        if x_first:
            first.append((cells, swap(cells, "bins", 1, 0)))
        else:
            first.append((cells, swap(cells, "bins", 2, 0), swap(cells, "bins", 2, 1)))
    done = moved[1]
    sums = [[], []]
    for (far, low, high, x_first), got in zip(CHUNKS, first):
        cells = got[0]
        if x_first:
            pair = after(got[1], done)
            done = total(low, high, (send_0[0], cells), (send_0[1], pair))
            r0 = swap(done, "bins", 2, 0)
            r1 = swap(total(low, high, (send_1[0], cells), (send_1[1], pair)), "bins", 2, 1)
            terms = ((on_self, cells), (from_pair, pair), (None, r0), (None, r1))
        else:
            z0, z1 = got[1:]
            z0 = after(z0, done)
            used = jnp.where(uses_0, z0, z1)
            done = total(low, high, (pair_own, cells), (pair_far, used))
            pair = swap(done, "bins", 1, 0)
            terms = ((on_self, cells), (far_0, z0), (far_1, z1), (None, pair))
        sums[far].append((low, high, terms))

    result = None
    for far in (0, 1):
        parts = []
        for low, high, terms in sorted(sums[far], key=lambda item: item[0]):
            terms = terms[:-1] + ((None, after(terms[-1][1], done)),)
            parts.append(total(low, high, *terms))
        result = done = collide(far == 0, jnp.concatenate(parts, 1), both, conc.shape, result)
    return result


def solution(mesh):
    placed = (
        P("bins", None, "xy", None),
        P("bins", "xy", None),
        P("bins", "xy", None),
        P("xy", None),
        P(),
        P(),
        P(),
        P(),
        P(),
    )
    return jax.shard_map(
        local, mesh=mesh, in_specs=placed, out_specs=P("bins", None, "xy", None), check_vma=False
    )
```

```python
import functools

import jax
import jax.numpy as jnp
from jax import lax
from jax.experimental import pallas as pl
from jax.experimental.pallas import tpu as pltpu
from jax.sharding import PartitionSpec as P

NB = 128
NCLS = 8

h_diffusion = 0.2
v_diffusion = 0.2
step_duration = 0.5
collide_scale = 2.0
SUBLANES = 8
EDGE = 2
CHUNKS = (((0, 0, 128, False),), ((1, 0, 128, True),))
VMEM = pl.BlockSpec(memory_space=pltpu.VMEM)
HBM = pl.BlockSpec(memory_space=pltpu.HBM)
ANY = pl.BlockSpec(memory_space=pl.ANY)
PARAMS = pltpu.CompilerParams(vmem_limit_bytes=8 << 20)


def in_vmem(*values):
    return [pltpu.with_memory_space_constraint(value, pltpu.VMEM) for value in values]


def in_hbm(*values):
    return [pltpu.with_memory_space_constraint(value, pltpu.HBM) for value in values]


def odd_core():
    return lax.axis_index("xy") % 2 == 1


def by_parity(body):
    odd = odd_core()
    pl.when(odd)(functools.partial(body, True))
    pl.when(jnp.logical_not(odd))(functools.partial(body, False))


def exchange(value, partner):
    bands = lax.axis_size("xy")
    pairs = []
    for level in range(lax.axis_size("bins")):
        for band in range(bands):
            to_level, to_band = partner(level, band)
            pairs.append((level * bands + band, to_level * bands + to_band))
    return lax.ppermute(value, ("bins", "xy"), pairs)


def swap_core(value):
    return exchange(value, lambda level, band: (level, band ^ 1))


def swap_chip(value):
    bands = lax.axis_size("xy")

    def partner(level, band):
        to = band + 1 if band % 2 else band - 1
        return (level, to) if 0 <= to < bands else (level ^ 1, band)

    return exchange(value, partner)


def swap_pair(value):
    return exchange(value, lambda level, band: (level ^ 1, band))


def swap_far(value, parity):
    levels = lax.axis_size("bins")

    def partner(level, band):
        to = level + 2 if level // 2 % 2 == parity else level - 2
        return (to, band) if 0 <= to < levels else (level, band ^ 1)

    return exchange(value, partner)


def load_kernel(conc, vel_x, vel_y, mask, rows, near, *refs):
    far, (flow, mask_rows, sems) = refs[:-3], refs[-3:]
    count, bins, _ = rows.shape
    part = bins // len(far)

    def body(odd):
        near_at, far_at = (0, count - EDGE) if odd else (count - EDGE, 0)
        copies = [pltpu.make_async_copy(mask, mask_rows, sems.at[0])]
        copies.append(pltpu.make_async_copy(vel_x.at[0], flow.at[0], sems.at[1]))
        copies.append(pltpu.make_async_copy(vel_y.at[0], flow.at[1], sems.at[2]))
        edges = [(near, near_at, 0, bins)] + [(ref, far_at, i * part, part) for i, ref in enumerate(far)]
        for target, at, low, size in edges:
            for r in range(EDGE):
                copies.append(
                    pltpu.make_async_copy(
                        conc.at[0, pl.ds(low, size), at + r, :], target.at[r, pl.ds(0, size)], sems.at[len(copies)]
                    )
                )
        for r in range(count):
            copies.append(pltpu.make_async_copy(conc.at[0, :, r, :], rows.at[r], sems.at[len(copies)]))
        for copy in copies:
            copy.start()
        for copy in copies[:3]:
            copy.wait()
        flow[2] = mask_rows[...].astype(jnp.float32)
        for target, at, _, size in edges:
            end = at if at == 0 else count - 1
            for r in range(EDGE):
                target[r, size:, :] = jnp.zeros_like(target[r, size:, :])
            for i in range(3):
                target[0, size + i : size + i + 1, :] = flow[i, end : end + 1, :]
        for copy in copies[3:]:
            copy.wait()

    by_parity(body)


def load(conc, vel_x, vel_y, mask, parts):
    _, bins, count, cols = conc.shape

    def edge(size):
        return pltpu.VMEM((EDGE, size + SUBLANES, cols), jnp.float32)

    rows, near, *far, flow = pl.pallas_call(
        load_kernel,
        out_shape=(
            pltpu.VMEM((count, bins, cols), jnp.float32),
            edge(bins),
            *[edge(bins // parts)] * parts,
            pltpu.VMEM((3, count, cols), jnp.float32),
        ),
        in_specs=[HBM] * 4,
        out_specs=(VMEM,) * (3 + parts),
        scratch_shapes=[
            pltpu.VMEM((count, cols), jnp.int32),
            pltpu.SemaphoreType.DMA((3 + EDGE * (1 + parts) + count,)),
        ],
        compiler_params=PARAMS,
    )(*in_hbm(conc, vel_x, vel_y, mask))
    return rows, near, far, flow


def horizontal_kernel(near, low, rows_ref, halo_ref, flow_ref, *refs):
    out_ref, scale_ref = refs[-2:]
    count, _, cols = rows_ref.shape
    bins = out_ref.shape[1]
    column = lax.broadcasted_iota(jnp.int32, (1, cols), 1)
    block = 4 * SUBLANES

    def body(odd):
        first = odd == near
        base = 0 if first else count - 4

        def row(i):
            if first:
                return (halo_ref, i) if i < EDGE else (rows_ref, i - EDGE)
            return (rows_ref, base + i) if i < 4 else (halo_ref, i - 4)

        band = lax.axis_index("xy")
        outside = jnp.logical_and(not near, jnp.logical_or(band == 0, band == lax.axis_size("xy") - 1))
        inside = jnp.where(outside, 0.0, 1.0)
        for i in range(1, 5):
            ref, at = row(i)
            if ref is halo_ref:
                aux = halo_ref[0, bins : bins + SUBLANES, :]
                x, y, water = aux[0:1], aux[1:2], aux[2:3] * inside
            else:
                x, y, water = (flow_ref[part, at : at + 1, :] for part in range(3))
            x, y = 0.5 * x, 0.5 * y
            east = inside if i == 3 and not first else 1.0
            west = inside if i == 2 and first else 1.0
            parts = (
                water * (1.0 - 4.0 * h_diffusion),
                water * (h_diffusion - x) * east,
                water * (h_diffusion + x) * west,
                jnp.where(column == cols - 1, 0.0, water * (h_diffusion - y)),
                jnp.where(column == 0, 0.0, water * (h_diffusion + y)),
            )
            for number, part in enumerate(parts):
                scale_ref[i - 1, number] = jnp.broadcast_to(part, (SUBLANES, cols))

        def step(cells, i):
            own, east, west, north, south = (
                jnp.concatenate([scale_ref[i - 1, number]] * (block // SUBLANES), 0) for number in range(5)
            )
            here = cells[i]
            return (
                own * here
                + east * cells[i + 1]
                + west * cells[i - 1]
                + north * pltpu.roll(here, cols - 1, 1)
                + south * pltpu.roll(here, 1, 1)
            )

        for at in range(0, bins, block):
            cells = {}
            for i in range(6):
                ref, place = row(i)
                cells[i] = ref[place, pl.ds(at if ref is halo_ref else low + at, block), :]
            once = {i: step(cells, i) for i in range(1, 5)}
            for i in range(EDGE):
                out_ref[i, pl.ds(at, block), :] = step(once, EDGE + i)

    by_parity(body)


def horizontal(near, rows, halo, flow, low, size, before=()):
    cols = rows.shape[2]
    return pl.pallas_call(
        functools.partial(horizontal_kernel, near, low),
        out_shape=pltpu.VMEM((EDGE, size, cols), jnp.float32),
        in_specs=[VMEM] * 3 + [ANY] * len(before),
        out_specs=VMEM,
        scratch_shapes=[pltpu.VMEM((4, 5, SUBLANES, cols), jnp.float32)],
        cost_estimate=pl.CostEstimate(flops=6 * 9 * size * cols, bytes_accessed=32 * size * cols, transcendentals=0),
        compiler_params=PARAMS,
    )(*in_vmem(rows, halo, flow, *before))


def weigh(table_ref, low, terms):
    out = None
    for column, cells in terms:
        part = table_ref[low : low + cells.shape[0], column : column + 1] * cells
        out = part if out is None else out + part
    return out


def combine_kernel(low, sums, width, table_ref, *refs):
    cells, outs = refs[:width], refs[len(refs) - len(sums) :]
    for r in range(EDGE):
        for terms, out in zip(sums, outs):
            out[r] = weigh(table_ref, low, [(column, cells[i][r]) for i, column in enumerate(terms)])


def combine(table, low, cells, sums, before=()):
    outs = pl.pallas_call(
        functools.partial(combine_kernel, low, sums, len(cells)),
        out_shape=(pltpu.VMEM(cells[0].shape, jnp.float32),) * len(sums),
        in_specs=[VMEM] * (1 + len(cells)) + [ANY] * len(before),
        out_specs=(VMEM,) * len(sums),
        cost_estimate=pl.CostEstimate(flops=6 * cells[0].size, bytes_accessed=20 * cells[0].size, transcendentals=0),
        compiler_params=PARAMS,
    )(*in_vmem(table, *cells, *before))
    return list(outs)


def split(value):
    high = value.astype(jnp.bfloat16)
    return high, (value - high.astype(jnp.float32)).astype(jnp.bfloat16)


def collide_kernel(near, parts, table_ref, both_ref, *refs):
    out_ref, done_ref, sems = refs[-3:]
    count = out_ref.shape[2]

    def body(odd):
        at = 0 if odd == near else count - EDGE
        copies = []
        for r in range(EDGE):
            first, pieces = 0, []
            for low, columns in parts:
                cells = refs[first : first + len(columns)]
                first += len(columns)
                pieces.append(weigh(table_ref, low, [(column, ref[r]) for column, ref in zip(columns, cells)]))
            cells = jnp.concatenate(pieces, 0)
            high, low = split(cells)
            sums = jnp.dot(
                both_ref[...], jnp.concatenate([high, low, high], 0), preferred_element_type=jnp.float32
            )
            done_ref[r] = cells + cells * sums[:NB] + sums[NB:]
            copies.append(pltpu.make_async_copy(done_ref.at[r], out_ref.at[0, :, at + r, :], sems.at[r]))
            copies[-1].start()
        for copy in copies:
            copy.wait()

    by_parity(body)


def collide(near, table, both, parts, shape, before=None):
    rest = () if before is None else (before,)
    cells = [value for _, terms in parts for _, value in terms]
    parts = [(low, [column for column, _ in terms]) for low, terms in parts]
    cols = shape[3]
    return pl.pallas_call(
        functools.partial(collide_kernel, near, parts),
        out_shape=pltpu.HBM(shape, jnp.float32),
        in_specs=[VMEM] * (2 + len(cells)) + [HBM] * len(rest),
        out_specs=HBM,
        input_output_aliases={2 + len(cells): 0} if rest else {},
        scratch_shapes=[pltpu.VMEM((EDGE, NB, cols), jnp.float32), pltpu.SemaphoreType.DMA((EDGE,))],
        cost_estimate=pl.CostEstimate(
            flops=12 * NB * NB * EDGE * cols, bytes_accessed=24 * EDGE * NB * cols, transcendentals=0
        ),
        compiler_params=PARAMS,
    )(*in_vmem(table, both, *cells), *in_hbm(*rest))


def local(
    conc,
    vel_x,
    vel_y,
    sea_mask,
    settle,
    size_bin_kernel_class,
    aggregate_upward_factor,
    agg_down,
    break_rate,
):
    rows, near_edge, far_edges, flow = load(conc, vel_x, vel_y, sea_mask, 1)
    halo_core = swap_core(near_edge)
    halo_chip = [swap_chip(edge) for edge in far_edges]
    part = NB // 1
    near = horizontal(True, rows, halo_core, flow, 0, NB)
    far = []
    for i in reversed(range(1)):
        far.insert(0, horizontal(False, rows, halo_chip[i], flow, i * part, part, (far or [near])[:1]))

    def transported(is_far, low, high):
        if not is_far:
            return near[:, low:high]
        if high - low > part:
            return jnp.concatenate(far, 1)
        return far[low // part][:, low % part : low % part + high - low]

    levels = lax.axis_size("bins")
    k = lax.axis_index("bins")
    odd = k % 2 == 1
    high_z = (k // 2) % 2 == 1
    fall = settle + v_diffusion
    rise = jnp.full_like(settle, v_diffusion)

    def keep(level):
        inner = (level > 0).astype(jnp.float32) + (level < levels - 1).astype(jnp.float32)
        return 1.0 - settle - v_diffusion * inner

    inner = (k > 0).astype(jnp.float32) + (k < levels - 1).astype(jnp.float32)
    on_self = keep(k) * keep(k) + inner * fall * rise
    up2, down2 = fall * fall, rise * rise
    zero = jnp.zeros_like(settle)
    up_pair = jnp.where(odd, zero, fall * (keep(k + 2) + keep(k + 1)))
    down_pair = jnp.where(odd, rise * (keep(k - 2) + keep(k - 1)), zero)
    send_0 = (jnp.where(high_z, down2, up2), jnp.where(high_z, down_pair, up_pair))
    send_1 = (jnp.where(high_z, up2, down2), jnp.where(high_z, up_pair, down_pair))
    from_pair = jnp.where(odd, fall * (keep(k) + keep(k - 1)), rise * (keep(k) + keep(k + 1)))
    pair_own = jnp.where(odd, rise * (keep(k - 1) + keep(k)), fall * (keep(k + 1) + keep(k)))
    pair_far = jnp.where(odd, fall * (keep(k - 1) + keep(k - 2)), rise * (keep(k + 1) + keep(k + 2)))
    below, above = (k >= 2).astype(jnp.float32), (k + 2 < levels).astype(jnp.float32)
    there_0, there_1 = jnp.where(high_z, below, above), jnp.where(high_z, above, below)
    far_0 = jnp.where(high_z, up2, down2) * there_0
    far_1 = jnp.where(high_z, down2, up2) * there_1
    pair_far = pair_far * jnp.where(odd, below, above)
    uses_0 = odd == high_z

    onehot = (size_bin_kernel_class[:, None] == jnp.arange(NCLS)[None, :]).astype(jnp.float32)

    def lookup(table):
        return jnp.sum(onehot * table[None, :], 1)

    up_rate = lookup(aggregate_upward_factor)
    down_rate = lookup(agg_down)
    brk_rate = lookup(break_rate)
    index = jnp.arange(NB)
    i, j = index[None, :], index[:, None]
    weight = 1.0 / jnp.maximum(index, 1).astype(jnp.float32)
    pairs = jnp.where(i < j, down_rate[:, None] * up_rate[None, :], 0.0) - jnp.where(
        i > j, up_rate[:, None] * down_rate[None, :], 0.0
    )
    pieces = jnp.where(i > j, (brk_rate * weight)[None, :], 0.0) - jnp.where(
        (i == j) & (j >= 1), brk_rate[:, None], 0.0
    )
    both = jnp.concatenate([pairs * (step_duration * collide_scale / NB), pieces * step_duration], 0)

    high = lax.reduce_precision(both, 8, 7)
    low = both - high
    both = jnp.concatenate([high, high, low], 1).astype(jnp.bfloat16)

    columns = [
        send_0[0], send_0[1], send_1[0], send_1[1], on_self, from_pair, there_0 + zero, there_1 + zero,
        pair_own, jnp.where(uses_0, pair_far, zero), jnp.where(uses_0, zero, pair_far), far_0, far_1, zero + 1.0,
    ]
    table = jnp.pad(jnp.stack(columns, 1), ((0, 0), (0, 128 - len(columns))))

    first = []
    for group in CHUNKS:
        for is_far, low, high, x_first in group:
            cells = transported(is_far, low, high)
            if x_first:
                first.append((cells, swap_pair(cells)))
            elif True:
                z1 = swap_far(cells, 1)
                first.append((cells, swap_far(cells, 0), z1))
            else:
                first.append((cells, swap_far(cells, 0), swap_far(cells, 1)))
    parts = [[], []]
    before = ()
    for group in CHUNKS:
        came = [first.pop(0) for _ in group]
        if len(group) > 1:
            came = lax.optimization_barrier(came)
        for (is_far, low, high, x_first), cells in zip(group, came):
            if x_first:
                sends = combine(table, low, cells, ((0, 1), (2, 3)), before)
                if True:
                    r1 = swap_far(sends[1], 1)
                    r0 = swap_far(sends[0], 0)
                else:
                    r0 = swap_far(sends[0], 0)
                    r1 = swap_far(sends[1], 1)
                terms = [(4, cells[0]), (5, cells[1]), (6, r0), (7, r1)]
            else:
                sends = combine(table, low, cells, ((8, 9, 10),), before)
                terms = [(4, cells[0]), (11, cells[1]), (12, cells[2]), (13, swap_pair(sends[0]))]
            before = tuple(sends[:1])
            parts[is_far].append((low, terms))
    result = None
    for is_far in (0, 1):
        result = collide(
            not is_far, table, both, sorted(parts[is_far], key=lambda item: item[0]), conc.shape, result
        )
    return result


def solution(mesh):
    placed = (
        P("bins", None, "xy", None),
        P("bins", "xy", None),
        P("bins", "xy", None),
        P("xy", None),
        P(),
        P(),
        P(),
        P(),
        P(),
    )
    return jax.shard_map(
        local, mesh=mesh, in_specs=placed, out_specs=P("bins", None, "xy", None), check_vma=False
    )
```

```python
import functools

import jax
import jax.numpy as jnp
from jax import lax
from jax.experimental import pallas as pl
from jax.experimental.pallas import tpu as pltpu
from jax.sharding import PartitionSpec as P

NB = 128
NCLS = 8

h_diffusion = 0.2
v_diffusion = 0.2
step_duration = 0.5
collide_scale = 2.0
SUBLANES = 8
EDGE = 2
CHUNKS = (((0, 0, 128, False),), ((1, 0, 128, True),))
VMEM = pl.BlockSpec(memory_space=pltpu.VMEM)
HBM = pl.BlockSpec(memory_space=pltpu.HBM)
ANY = pl.BlockSpec(memory_space=pl.ANY)
PARAMS = pltpu.CompilerParams(vmem_limit_bytes=8 << 20)


def in_vmem(*values):
    return [pltpu.with_memory_space_constraint(value, pltpu.VMEM) for value in values]


def in_hbm(*values):
    return [pltpu.with_memory_space_constraint(value, pltpu.HBM) for value in values]


def odd_core():
    return lax.axis_index("xy") % 2 == 1


def by_parity(body):
    odd = odd_core()
    pl.when(odd)(functools.partial(body, True))
    pl.when(jnp.logical_not(odd))(functools.partial(body, False))


def exchange(value, partner):
    bands = lax.axis_size("xy")
    pairs = []
    for level in range(lax.axis_size("bins")):
        for band in range(bands):
            to_level, to_band = partner(level, band)
            pairs.append((level * bands + band, to_level * bands + to_band))
    return lax.ppermute(value, ("bins", "xy"), pairs)


def swap_core(value):
    return exchange(value, lambda level, band: (level, band ^ 1))


def swap_chip(value):
    bands = lax.axis_size("xy")

    def partner(level, band):
        to = band + 1 if band % 2 else band - 1
        return (level, to) if 0 <= to < bands else (level ^ 1, band)

    return exchange(value, partner)


def swap_pair(value):
    return exchange(value, lambda level, band: (level ^ 1, band))


def swap_far(value, parity):
    levels = lax.axis_size("bins")

    def partner(level, band):
        to = level + 2 if level // 2 % 2 == parity else level - 2
        return (to, band) if 0 <= to < levels else (level, band ^ 1)

    return exchange(value, partner)


def load_kernel(conc, vel_x, vel_y, mask, near, far, flow, mask_rows, sems):
    _, bins, count, _ = conc.shape

    def body(odd):
        near_at, far_at = (0, count - EDGE) if odd else (count - EDGE, 0)
        copies = []
        for target, at in ((far, far_at), (near, near_at)):
            for r in range(EDGE):
                copies.append(
                    pltpu.make_async_copy(
                        conc.at[0, :, at + r, :], target.at[r, pl.ds(0, bins)], sems.at[len(copies)]
                    )
                )
        for source, target in ((mask, mask_rows), (vel_x.at[0], flow.at[0]), (vel_y.at[0], flow.at[1])):
            copies.append(pltpu.make_async_copy(source, target, sems.at[len(copies)]))
        for copy in copies:
            copy.start()
        for target in (far, near):
            for r in range(EDGE):
                target[r, bins:, :] = jnp.zeros_like(target[r, bins:, :])
        for copy in copies[2 * EDGE :]:
            copy.wait()
        flow[2] = mask_rows[...].astype(jnp.float32)
        for target, at in ((far, far_at), (near, near_at)):
            end = 0 if at == 0 else count - 1
            for i in range(3):
                target[0, bins + i : bins + i + 1, :] = flow[i, end : end + 1, :]
        for copy in copies[: 2 * EDGE]:
            copy.wait()

    by_parity(body)


def load(conc, vel_x, vel_y, mask):
    _, bins, count, cols = conc.shape
    assert count == 2 * EDGE
    edge = pltpu.VMEM((EDGE, bins + SUBLANES, cols), jnp.float32)
    return pl.pallas_call(
        load_kernel,
        out_shape=(edge, edge, pltpu.VMEM((3, count, cols), jnp.float32)),
        in_specs=[HBM] * 4,
        out_specs=(VMEM,) * 3,
        scratch_shapes=[pltpu.VMEM((count, cols), jnp.int32), pltpu.SemaphoreType.DMA((3 + 2 * EDGE,))],
        compiler_params=PARAMS,
    )(*in_hbm(conc, vel_x, vel_y, mask))


def horizontal_kernel(near, own_ref, other_ref, halo_ref, flow_ref, *refs):
    out_ref, scale_ref = refs[-2:]
    _, bins, cols = out_ref.shape
    count = flow_ref.shape[1]
    column = lax.broadcasted_iota(jnp.int32, (1, cols), 1)
    block = 16 * SUBLANES

    def body(odd):
        first = odd == near
        order = (halo_ref, own_ref, other_ref) if first else (other_ref, own_ref, halo_ref)
        base = 2 if first else 0

        band = lax.axis_index("xy")
        outside = jnp.logical_and(not near, jnp.logical_or(band == 0, band == lax.axis_size("xy") - 1))
        inside = jnp.where(outside, 0.0, 1.0)
        for i in range(1, 5):
            if order[i // EDGE] is halo_ref:
                aux = halo_ref[0, bins : bins + SUBLANES, :]
                x, y, water = aux[0:1], aux[1:2], aux[2:3] * inside
            else:
                at = i - base
                x, y, water = (flow_ref[part, at : at + 1, :] for part in range(3))
            x, y = 0.5 * x, 0.5 * y
            east = inside if i == 3 and not first else 1.0
            west = inside if i == 2 and first else 1.0
            parts = (
                water * (1.0 - 4.0 * h_diffusion),
                water * (h_diffusion - x) * east,
                water * (h_diffusion + x) * west,
                jnp.where(column == cols - 1, 0.0, water * (h_diffusion - y)),
                jnp.where(column == 0, 0.0, water * (h_diffusion + y)),
            )
            for number, part in enumerate(parts):
                scale_ref[i - 1, number] = jnp.broadcast_to(part, (SUBLANES, cols))

        def step(cells, i):
            own, east, west, north, south = (
                jnp.concatenate([scale_ref[i - 1, number]] * (block // SUBLANES), 0) for number in range(5)
            )
            here = cells[i]
            return (
                own * here
                + east * cells[i + 1]
                + west * cells[i - 1]
                + north * pltpu.roll(here, cols - 1, 1)
                + south * pltpu.roll(here, 1, 1)
            )

        for at in range(0, bins, block):
            cells = {i: order[i // EDGE][i % EDGE, pl.ds(at, block), :] for i in range(6)}
            once = {i: step(cells, i) for i in range(1, 5)}
            for i in range(EDGE):
                out_ref[i, pl.ds(at, block), :] = step(once, EDGE + i)

    by_parity(body)


def horizontal(near, own, other, halo, flow, before=()):
    _, bins, cols = own.shape
    bins -= SUBLANES
    return pl.pallas_call(
        functools.partial(horizontal_kernel, near),
        out_shape=pltpu.VMEM((EDGE, bins, cols), jnp.float32),
        in_specs=[VMEM] * 4 + [ANY] * len(before),
        out_specs=VMEM,
        scratch_shapes=[pltpu.VMEM((4, 5, SUBLANES, cols), jnp.float32)],
        cost_estimate=pl.CostEstimate(flops=6 * 9 * bins * cols, bytes_accessed=32 * bins * cols, transcendentals=0),
        compiler_params=PARAMS,
    )(*in_vmem(own, other, halo, flow, *before))


def weigh(table_ref, low, terms):
    out = None
    for column, cells in terms:
        part = table_ref[low : low + cells.shape[0], column : column + 1] * cells
        out = part if out is None else out + part
    return out


def combine_kernel(low, sums, width, table_ref, *refs):
    cells, outs = refs[:width], refs[len(refs) - len(sums) :]
    for r in range(EDGE):
        for terms, out in zip(sums, outs):
            out[r] = weigh(table_ref, low, [(column, cells[i][r]) for i, column in enumerate(terms)])


def combine(table, low, cells, sums, before=()):
    outs = pl.pallas_call(
        functools.partial(combine_kernel, low, sums, len(cells)),
        out_shape=(pltpu.VMEM(cells[0].shape, jnp.float32),) * len(sums),
        in_specs=[VMEM] * (1 + len(cells)) + [ANY] * len(before),
        out_specs=(VMEM,) * len(sums),
        cost_estimate=pl.CostEstimate(flops=6 * cells[0].size, bytes_accessed=20 * cells[0].size, transcendentals=0),
        compiler_params=PARAMS,
    )(*in_vmem(table, *cells, *before))
    return list(outs)


def split(value):
    high = value.astype(jnp.bfloat16)
    return high, (value - high.astype(jnp.float32)).astype(jnp.bfloat16)


def collide_kernel(chunks, table_ref, both_ref, *refs):
    out_ref, done_ref, sems = refs[-3:]
    count, cols = out_ref.shape[2:]

    def body(odd):
        copies, first = [], 0
        for near, parts in chunks:
            at = 0 if odd == near else count - EDGE
            rows = [[] for _ in range(EDGE)]
            for low, columns in parts:
                cells = refs[first : first + len(columns)]
                first += len(columns)
                for r in range(EDGE):
                    rows[r].append(weigh(table_ref, low, [(column, ref[r]) for column, ref in zip(columns, cells)]))
            cells = jnp.concatenate([jnp.concatenate(pieces, 0) for pieces in rows], 1)
            high, low = split(cells)
            sums = jnp.dot(both_ref[...], jnp.concatenate([high, low, high], 0), preferred_element_type=jnp.float32)
            result = cells + cells * sums[:NB] + sums[NB:]
            for r in range(EDGE):
                slot = len(copies)
                done_ref[slot] = result[:, r * cols : (r + 1) * cols]
                copies.append(pltpu.make_async_copy(done_ref.at[slot], out_ref.at[0, :, at + r, :], sems.at[slot]))
                copies[-1].start()
        for copy in copies:
            copy.wait()

    by_parity(body)


def collide(table, both, chunks, shape, before=None):
    rest = () if before is None else (before,)
    cells = [value for _, parts in chunks for _, terms in parts for _, value in terms]
    chunks = [(near, [(low, [column for column, _ in terms]) for low, terms in parts]) for near, parts in chunks]
    rows, cols = EDGE * len(chunks), shape[3]
    return pl.pallas_call(
        functools.partial(collide_kernel, chunks),
        out_shape=pltpu.HBM(shape, jnp.float32),
        in_specs=[VMEM] * (2 + len(cells)) + [HBM] * len(rest),
        out_specs=HBM,
        input_output_aliases={2 + len(cells): 0} if rest else {},
        scratch_shapes=[pltpu.VMEM((rows, NB, cols), jnp.float32), pltpu.SemaphoreType.DMA((rows,))],
        cost_estimate=pl.CostEstimate(
            flops=12 * NB * NB * rows * cols, bytes_accessed=24 * rows * NB * cols, transcendentals=0
        ),
        compiler_params=PARAMS,
    )(*in_vmem(table, both, *cells), *in_hbm(*rest))


def local(
    conc,
    vel_x,
    vel_y,
    sea_mask,
    settle,
    size_bin_kernel_class,
    aggregate_upward_factor,
    agg_down,
    break_rate,
):
    near_edge, far_edge, flow = load(conc, vel_x, vel_y, sea_mask)
    halo_chip = swap_chip(far_edge)
    halo_core = swap_core(near_edge)
    near = horizontal(True, near_edge, far_edge, halo_core, flow)
    far = horizontal(False, far_edge, near_edge, halo_chip, flow, (near,))

    def transported(is_far, low, high):
        return (near, far)[is_far][:, low:high]

    levels = lax.axis_size("bins")
    k = lax.axis_index("bins")
    odd = k % 2 == 1
    high_z = (k // 2) % 2 == 1
    fall = settle + v_diffusion
    rise = jnp.full_like(settle, v_diffusion)

    def keep(level):
        inner = (level > 0).astype(jnp.float32) + (level < levels - 1).astype(jnp.float32)
        return 1.0 - settle - v_diffusion * inner

    inner = (k > 0).astype(jnp.float32) + (k < levels - 1).astype(jnp.float32)
    on_self = keep(k) * keep(k) + inner * fall * rise
    up2, down2 = fall * fall, rise * rise
    zero = jnp.zeros_like(settle)
    up_pair = jnp.where(odd, zero, fall * (keep(k + 2) + keep(k + 1)))
    down_pair = jnp.where(odd, rise * (keep(k - 2) + keep(k - 1)), zero)
    send_0 = (jnp.where(high_z, down2, up2), jnp.where(high_z, down_pair, up_pair))
    send_1 = (jnp.where(high_z, up2, down2), jnp.where(high_z, up_pair, down_pair))
    from_pair = jnp.where(odd, fall * (keep(k) + keep(k - 1)), rise * (keep(k) + keep(k + 1)))
    pair_own = jnp.where(odd, rise * (keep(k - 1) + keep(k)), fall * (keep(k + 1) + keep(k)))
    pair_far = jnp.where(odd, fall * (keep(k - 1) + keep(k - 2)), rise * (keep(k + 1) + keep(k + 2)))
    below, above = (k >= 2).astype(jnp.float32), (k + 2 < levels).astype(jnp.float32)
    there_0, there_1 = jnp.where(high_z, below, above), jnp.where(high_z, above, below)
    far_0 = jnp.where(high_z, up2, down2) * there_0
    far_1 = jnp.where(high_z, down2, up2) * there_1
    pair_far = pair_far * jnp.where(odd, below, above)
    uses_0 = odd == high_z

    onehot = (size_bin_kernel_class[:, None] == jnp.arange(NCLS)[None, :]).astype(jnp.float32)

    def lookup(table):
        return jnp.sum(onehot * table[None, :], 1)

    up_rate = lookup(aggregate_upward_factor)
    down_rate = lookup(agg_down)
    brk_rate = lookup(break_rate)
    index = jnp.arange(NB)
    i, j = index[None, :], index[:, None]
    weight = 1.0 / jnp.maximum(index, 1).astype(jnp.float32)
    pairs = jnp.where(i < j, down_rate[:, None] * up_rate[None, :], 0.0) - jnp.where(
        i > j, up_rate[:, None] * down_rate[None, :], 0.0
    )
    pieces = jnp.where(i > j, (brk_rate * weight)[None, :], 0.0) - jnp.where(
        (i == j) & (j >= 1), brk_rate[:, None], 0.0
    )
    both = jnp.concatenate([pairs * (step_duration * collide_scale / NB), pieces * step_duration], 0)

    high = lax.reduce_precision(both, 8, 7)
    low = both - high
    both = jnp.concatenate([high, high, low], 1).astype(jnp.bfloat16)

    columns = [
        send_0[0], send_0[1], send_1[0], send_1[1], on_self, from_pair, there_0 + zero, there_1 + zero,
        pair_own, jnp.where(uses_0, pair_far, zero), jnp.where(uses_0, zero, pair_far), far_0, far_1, zero + 1.0,
    ]
    table = jnp.pad(jnp.stack(columns, 1), ((0, 0), (0, 128 - len(columns))))

    first = []
    for group in CHUNKS:
        for is_far, low, high, x_first in group:
            cells = transported(is_far, low, high)
            if x_first:
                first.append((cells, swap_pair(cells)))
            elif True:
                z1 = swap_far(cells, 1)
                first.append((cells, swap_far(cells, 0), z1))
            else:
                first.append((cells, swap_far(cells, 0), swap_far(cells, 1)))
    parts = [[], []]
    before = ()
    for group in CHUNKS:
        came = [first.pop(0) for _ in group]
        if len(group) > 1:
            came = lax.optimization_barrier(came)
        for (is_far, low, high, x_first), cells in zip(group, came):
            if x_first:
                sends = combine(table, low, cells, ((0, 1), (2, 3)), before)
                if True:
                    r1 = swap_far(sends[1], 1)
                    r0 = swap_far(sends[0], 0)
                else:
                    r0 = swap_far(sends[0], 0)
                    r1 = swap_far(sends[1], 1)
                terms = [(4, cells[0]), (5, cells[1]), (6, r0), (7, r1)]
            else:
                sends = combine(table, low, cells, ((8, 9, 10),), before)
                terms = [(4, cells[0]), (11, cells[1]), (12, cells[2]), (13, swap_pair(sends[0]))]
            before = tuple(sends[:1])
            parts[is_far].append((low, terms))
    chunks = [(not is_far, sorted(parts[is_far], key=lambda item: item[0])) for is_far in (0, 1)]
    half = collide(table, both, chunks[:1], conc.shape)
    return collide(table, both, chunks[1:], conc.shape, half)


def solution(mesh):
    placed = (
        P("bins", None, "xy", None),
        P("bins", "xy", None),
        P("bins", "xy", None),
        P("xy", None),
        P(),
        P(),
        P(),
        P(),
        P(),
    )
    return jax.shard_map(
        local, mesh=mesh, in_specs=placed, out_specs=P("bins", None, "xy", None), check_vma=False
    )
```

```python
import functools

import jax
import jax.numpy as jnp
from jax import lax
from jax.experimental import pallas as pl
from jax.experimental.pallas import tpu as pltpu
from jax.sharding import PartitionSpec as P

NB = 128
NCLS = 8

h_diffusion = 0.2
v_diffusion = 0.2
step_duration = 0.5
collide_scale = 2.0
SUBLANES = 8
EDGE = 2
PARTS = 1
VMEM = pl.BlockSpec(memory_space=pltpu.VMEM)
HBM = pl.BlockSpec(memory_space=pltpu.HBM)
ANY = pl.BlockSpec(memory_space=pl.ANY)
PARAMS = pltpu.CompilerParams(vmem_limit_bytes=8 << 20)


def in_vmem(*values):
    return [pltpu.with_memory_space_constraint(value, pltpu.VMEM) for value in values]


def in_hbm(*values):
    return [pltpu.with_memory_space_constraint(value, pltpu.HBM) for value in values]


def odd_core():
    return lax.axis_index("xy") % 2 == 1


def by_parity(body):
    odd = odd_core()
    pl.when(odd)(functools.partial(body, True))
    pl.when(jnp.logical_not(odd))(functools.partial(body, False))


def exchange(value, partner):
    bands = lax.axis_size("xy")
    pairs = []
    for level in range(lax.axis_size("bins")):
        for band in range(bands):
            to_level, to_band = partner(level, band)
            pairs.append((level * bands + band, to_level * bands + to_band))
    return lax.ppermute(value, ("bins", "xy"), pairs)


def swap_core(value):
    return exchange(value, lambda level, band: (level, band ^ 1))


def swap_chip(value):
    bands = lax.axis_size("xy")

    def partner(level, band):
        to = band + 1 if band % 2 else band - 1
        return (level, to) if 0 <= to < bands else (level ^ 2, band)

    return exchange(value, partner)


def swap_pair(value):
    return exchange(value, lambda level, band: (level ^ 1, band))


def swap_far(value, parity):
    levels = lax.axis_size("bins")

    def partner(level, band):
        to = level + 2 if level // 2 % 2 == parity else level - 2
        return (to, band) if 0 <= to < levels else (level, band ^ 1)

    return exchange(value, partner)


def load_kernel(conc, vel_x, vel_y, mask, near, *refs):
    far, (flow, mask_rows, sems) = refs[:-3], refs[-3:]
    _, bins, count, _ = conc.shape
    part = bins // len(far)

    def body(odd):
        near_at, far_at = (0, count - EDGE) if odd else (count - EDGE, 0)
        edges = [(ref, far_at, i * part, part) for i, ref in enumerate(far)] + [(near, near_at, 0, bins)]
        copies = []
        for target, at, low, size in edges:
            for r in range(EDGE):
                copies.append(
                    pltpu.make_async_copy(
                        conc.at[0, pl.ds(low, size), at + r, :], target.at[r, pl.ds(0, size)], sems.at[len(copies)]
                    )
                )
        rows = len(copies)
        for source, target in ((mask, mask_rows), (vel_x.at[0], flow.at[0]), (vel_y.at[0], flow.at[1])):
            copies.append(pltpu.make_async_copy(source, target, sems.at[len(copies)]))
        for copy in copies:
            copy.start()
        for target, _, _, size in edges:
            for r in range(EDGE):
                target[r, size:, :] = jnp.zeros_like(target[r, size:, :])
        for copy in copies[rows:]:
            copy.wait()
        flow[2] = mask_rows[...].astype(jnp.float32)
        for target, at, _, size in edges:
            end = 0 if at == 0 else count - 1
            for i in range(3):
                target[0, size + i : size + i + 1, :] = flow[i, end : end + 1, :]
        for copy in copies[:rows]:
            copy.wait()

    by_parity(body)


def load(conc, vel_x, vel_y, mask):
    _, bins, count, cols = conc.shape
    assert count == 2 * EDGE

    def edge(size):
        return pltpu.VMEM((EDGE, size + SUBLANES, cols), jnp.float32)

    near, *far, flow = pl.pallas_call(
        load_kernel,
        out_shape=(edge(bins), *[edge(bins // PARTS)] * PARTS, pltpu.VMEM((3, count, cols), jnp.float32)),
        in_specs=[HBM] * 4,
        out_specs=(VMEM,) * (2 + PARTS),
        scratch_shapes=[
            pltpu.VMEM((count, cols), jnp.int32),
            pltpu.SemaphoreType.DMA((3 + EDGE * (1 + PARTS),)),
        ],
        compiler_params=PARAMS,
    )(*in_hbm(conc, vel_x, vel_y, mask))
    return near, far, flow


def horizontal_kernel(near, low, near_ref, *refs):
    far_refs, (halo_ref, flow_ref) = refs[: 1 if low is not None else PARTS], refs[1 if low is not None else PARTS :][:2]
    out_ref, scale_ref = refs[-2:]
    _, bins, cols = out_ref.shape
    share = NB // PARTS
    count = flow_ref.shape[1]
    column = lax.broadcasted_iota(jnp.int32, (1, cols), 1)
    block = 16 * SUBLANES

    def body(odd):
        first = odd == near
        order = ("halo", "own", "other") if first else ("other", "own", "halo")
        base = 2 if first else 0

        band = lax.axis_index("xy")
        outside = jnp.logical_and(not near, jnp.logical_or(band == 0, band == lax.axis_size("xy") - 1))
        inside = jnp.where(outside, 0.0, 1.0)
        for i in range(1, 5):
            if order[i // EDGE] == "halo":
                aux = halo_ref[0, bins : bins + SUBLANES, :]
                x, y, water = aux[0:1], aux[1:2], aux[2:3] * inside
            else:
                at = i - base
                x, y, water = (flow_ref[part, at : at + 1, :] for part in range(3))
            x, y = 0.5 * x, 0.5 * y
            east = inside if i == 3 and not first else 1.0
            west = inside if i == 2 and first else 1.0
            parts = (
                water * (1.0 - 4.0 * h_diffusion),
                water * (h_diffusion - x) * east,
                water * (h_diffusion + x) * west,
                jnp.where(column == cols - 1, 0.0, water * (h_diffusion - y)),
                jnp.where(column == 0, 0.0, water * (h_diffusion + y)),
            )
            for number, part in enumerate(parts):
                scale_ref[i - 1, number] = jnp.broadcast_to(part, (SUBLANES, cols))

        def step(cells, i):
            own, east, west, north, south = (
                jnp.concatenate([scale_ref[i - 1, number]] * (block // SUBLANES), 0) for number in range(5)
            )
            here = cells[i]
            return (
                own * here
                + east * cells[i + 1]
                + west * cells[i - 1]
                + north * pltpu.roll(here, cols - 1, 1)
                + south * pltpu.roll(here, 1, 1)
            )

        for at in range(0, bins, block):
            cells = {}
            for i in range(6):
                kind = order[i // EDGE]
                if kind == "halo":
                    ref, place = halo_ref, at
                elif (kind == "own") == near:
                    ref, place = near_ref, at + (low or 0)
                else:
                    ref, place = far_refs[at // share], at % share
                cells[i] = ref[i % EDGE, pl.ds(place, block), :]
            once = {i: step(cells, i) for i in range(1, 5)}
            for i in range(EDGE):
                out_ref[i, pl.ds(at, block), :] = step(once, EDGE + i)

    by_parity(body)


def horizontal(low, near, far, halo, flow, before=()):
    _, bins, cols = halo.shape
    bins -= SUBLANES
    return pl.pallas_call(
        functools.partial(horizontal_kernel, low is None, low),
        out_shape=pltpu.VMEM((EDGE, bins, cols), jnp.float32),
        in_specs=[VMEM] * (3 + len(far)) + [ANY] * len(before),
        out_specs=VMEM,
        scratch_shapes=[pltpu.VMEM((4, 5, SUBLANES, cols), jnp.float32)],
        cost_estimate=pl.CostEstimate(flops=6 * 9 * bins * cols, bytes_accessed=32 * bins * cols, transcendentals=0),
        compiler_params=PARAMS,
    )(*in_vmem(near, *far, halo, flow, *before))


def weigh(table_ref, low, terms):
    out = None
    for column, cells in terms:
        part = cells if column is None else table_ref[low : low + cells.shape[0], column : column + 1] * cells
        out = part if out is None else out + part
    return out


def combine_kernel(sums, width, table_ref, *refs):
    outs = refs[len(refs) - len(sums) :]
    low = 0
    while low < NB:
        cells, refs = refs[:width], refs[width:]
        size = cells[0].shape[1]
        for r in range(EDGE):
            for terms, out in zip(sums, outs):
                out[r, pl.ds(low, size)] = weigh(table_ref, low, [(at, cells[i][r]) for i, at in enumerate(terms)])
        low += size


def combine(table, parts, sums, before=()):
    cells = [value for part in parts for value in part]
    shape = (EDGE, NB, cells[0].shape[2])
    outs = pl.pallas_call(
        functools.partial(combine_kernel, sums, len(parts[0])),
        out_shape=(pltpu.VMEM(shape, jnp.float32),) * len(sums),
        in_specs=[VMEM] * (1 + len(cells)) + [ANY] * len(before),
        out_specs=(VMEM,) * len(sums),
        cost_estimate=pl.CostEstimate(
            flops=6 * NB * EDGE * shape[2], bytes_accessed=20 * NB * EDGE * shape[2], transcendentals=0
        ),
        compiler_params=PARAMS,
    )(*in_vmem(table, *cells, *before))
    return list(outs)


def split(value):
    high = value.astype(jnp.bfloat16)
    return high, (value - high.astype(jnp.float32)).astype(jnp.bfloat16)


def collide_kernel(chunks, table_ref, both_ref, *refs):
    out_ref, done_ref, sems = refs[-3:]
    count, cols = out_ref.shape[2:]

    def body(odd):
        copies, first = [], 0
        for near, parts in chunks:
            at = 0 if odd == near else count - EDGE
            rows = [[] for _ in range(EDGE)]
            for low, columns in parts:
                cells = refs[first : first + len(columns)]
                first += len(columns)
                for r in range(EDGE):
                    rows[r].append(weigh(table_ref, low, [(column, ref[r]) for column, ref in zip(columns, cells)]))
            cells = jnp.concatenate([jnp.concatenate(pieces, 0) for pieces in rows], 1)
            high, low = split(cells)
            sums = jnp.dot(both_ref[...], jnp.concatenate([high, low, high], 0), preferred_element_type=jnp.float32)
            result = cells + cells * sums[:NB] + sums[NB:]
            for r in range(EDGE):
                slot = len(copies)
                done_ref[slot] = result[:, r * cols : (r + 1) * cols]
                copies.append(pltpu.make_async_copy(done_ref.at[slot], out_ref.at[0, :, at + r, :], sems.at[slot]))
                copies[-1].start()
        for copy in copies:
            copy.wait()

    by_parity(body)


def collide(table, both, chunks, shape, before=None):
    rest = () if before is None else (before,)
    cells = [value for _, parts in chunks for _, terms in parts for _, value in terms]
    chunks = [(near, [(low, [column for column, _ in terms]) for low, terms in parts]) for near, parts in chunks]
    rows, cols = EDGE * len(chunks), shape[3]
    return pl.pallas_call(
        functools.partial(collide_kernel, chunks),
        out_shape=pltpu.HBM(shape, jnp.float32),
        in_specs=[VMEM] * (2 + len(cells)) + [HBM] * len(rest),
        out_specs=HBM,
        input_output_aliases={2 + len(cells): 0} if rest else {},
        scratch_shapes=[pltpu.VMEM((rows, NB, cols), jnp.float32), pltpu.SemaphoreType.DMA((rows,))],
        cost_estimate=pl.CostEstimate(
            flops=12 * NB * NB * rows * cols, bytes_accessed=24 * rows * NB * cols, transcendentals=0
        ),
        compiler_params=PARAMS,
    )(*in_vmem(table, both, *cells), *in_hbm(*rest))


def local(
    conc,
    vel_x,
    vel_y,
    sea_mask,
    settle,
    size_bin_kernel_class,
    aggregate_upward_factor,
    agg_down,
    break_rate,
):
    near_edge, far_edges, flow = load(conc, vel_x, vel_y, sea_mask)
    halo_chip = [swap_chip(edge) for edge in far_edges]
    halo_core = swap_core(near_edge)
    near = horizontal(None, near_edge, far_edges, halo_core, flow)
    part = NB // PARTS
    far, before = [], (near,)
    for i, edge in enumerate(far_edges):
        far.append(horizontal(i * part, near_edge, [edge], halo_chip[i], flow, before))
        before = (far[-1],)

    levels = lax.axis_size("bins")
    k = lax.axis_index("bins")
    odd = k % 2 == 1
    high_z = (k // 2) % 2 == 1
    fall = settle + v_diffusion
    rise = jnp.full_like(settle, v_diffusion)

    def keep(level):
        inner = (level > 0).astype(jnp.float32) + (level < levels - 1).astype(jnp.float32)
        return 1.0 - settle - v_diffusion * inner

    inner = (k > 0).astype(jnp.float32) + (k < levels - 1).astype(jnp.float32)
    on_self = keep(k) * keep(k) + inner * fall * rise
    up2, down2 = fall * fall, rise * rise
    zero = jnp.zeros_like(settle)
    up_pair = jnp.where(odd, zero, fall * (keep(k + 2) + keep(k + 1)))
    down_pair = jnp.where(odd, rise * (keep(k - 2) + keep(k - 1)), zero)
    send_0 = (jnp.where(high_z, down2, up2), jnp.where(high_z, down_pair, up_pair))
    send_1 = (jnp.where(high_z, up2, down2), jnp.where(high_z, up_pair, down_pair))
    from_pair = jnp.where(odd, fall * (keep(k) + keep(k - 1)), rise * (keep(k) + keep(k + 1)))
    pair_own = jnp.where(odd, rise * (keep(k - 1) + keep(k)), fall * (keep(k + 1) + keep(k)))
    pair_far = jnp.where(odd, fall * (keep(k - 1) + keep(k - 2)), rise * (keep(k + 1) + keep(k + 2)))
    below, above = (k >= 2).astype(jnp.float32), (k + 2 < levels).astype(jnp.float32)
    there_0, there_1 = jnp.where(high_z, below, above), jnp.where(high_z, above, below)
    from_0 = jnp.where(high_z, up2, down2) * there_0
    from_1 = jnp.where(high_z, down2, up2) * there_1
    pair_far = pair_far * jnp.where(odd, below, above)
    uses_0 = odd == high_z

    onehot = (size_bin_kernel_class[:, None] == jnp.arange(NCLS)[None, :]).astype(jnp.float32)

    def lookup(table):
        return jnp.sum(onehot * table[None, :], 1)

    up_rate = lookup(aggregate_upward_factor)
    down_rate = lookup(agg_down)
    brk_rate = lookup(break_rate)
    index = jnp.arange(NB)
    i, j = index[None, :], index[:, None]
    weight = 1.0 / jnp.maximum(index, 1).astype(jnp.float32)
    matrix = jnp.where(i < j, down_rate[:, None] * up_rate[None, :], 0.0) - jnp.where(
        i > j, up_rate[:, None] * down_rate[None, :], 0.0
    )
    pieces = jnp.where(i > j, (brk_rate * weight)[None, :], 0.0) - jnp.where(
        (i == j) & (j >= 1), brk_rate[:, None], 0.0
    )
    both = jnp.concatenate([matrix * (step_duration * collide_scale / NB), pieces * step_duration], 0)

    high = lax.reduce_precision(both, 8, 7)
    low = both - high
    both = jnp.concatenate([high, high, low], 1).astype(jnp.bfloat16)

    columns = [
        send_0[0], send_0[1], send_1[0], send_1[1], on_self, from_pair, there_0 + zero, there_1 + zero,
        pair_own, jnp.where(uses_0, pair_far, zero), jnp.where(uses_0, zero, pair_far), from_0, from_1, zero + 1.0,
    ]
    table = jnp.pad(jnp.stack(columns, 1), ((0, 0), (0, 128 - len(columns))))

    far_1 = swap_far(near, 1)
    far_0 = swap_far(near, 0)
    pairs_far = [(cells, swap_pair(cells)) for cells in far]
    (send,) = combine(table, [(near, far_0, far_1)], ((8, 9, 10),))
    pair = swap_pair(send)
    sends = combine(table, pairs_far, ((0, 1),), (send,))
    sends += combine(table, pairs_far, ((2, 3), (4, 5)), (sends[0],))
    back_1 = swap_far(sends[1], 1)
    back_0 = swap_far(sends[0], 0)
    half = collide(table, both, [(True, [(0, [(4, near), (11, far_0), (12, far_1), (None, pair)])])], conc.shape)
    return collide(table, both, [(False, [(0, [(None, sends[2]), (6, back_0), (7, back_1)])])], conc.shape, half)


def solution(mesh):
    placed = (
        P("bins", None, "xy", None),
        P("bins", "xy", None),
        P("bins", "xy", None),
        P("xy", None),
        P(),
        P(),
        P(),
        P(),
        P(),
    )
    return jax.shard_map(
        local, mesh=mesh, in_specs=placed, out_specs=P("bins", None, "xy", None), check_vma=False
    )
```

```python
import functools

import jax
import jax.numpy as jnp
from jax import lax
from jax.experimental import pallas as pl
from jax.experimental.pallas import tpu as pltpu
from jax.sharding import PartitionSpec as P

NB = 128
NCLS = 8

h_diffusion = 0.2
v_diffusion = 0.2
step_duration = 0.5
collide_scale = 2.0
SUBLANES = 8
EDGE = 2
PARTS = 1
VMEM = pl.BlockSpec(memory_space=pltpu.VMEM)
HBM = pl.BlockSpec(memory_space=pltpu.HBM)
ANY = pl.BlockSpec(memory_space=pl.ANY)
PARAMS = pltpu.CompilerParams(vmem_limit_bytes=8 << 20)


def in_vmem(*values):
    return [pltpu.with_memory_space_constraint(value, pltpu.VMEM) for value in values]


def in_hbm(*values):
    return [pltpu.with_memory_space_constraint(value, pltpu.HBM) for value in values]


def odd_core():
    return lax.axis_index("xy") % 2 == 1


def by_parity(body):
    odd = odd_core()
    pl.when(odd)(functools.partial(body, True))
    pl.when(jnp.logical_not(odd))(functools.partial(body, False))


def exchange(value, partner):
    bands = lax.axis_size("xy")
    pairs = []
    for level in range(lax.axis_size("bins")):
        for band in range(bands):
            to_level, to_band = partner(level, band)
            pairs.append((level * bands + band, to_level * bands + to_band))
    return lax.ppermute(value, ("bins", "xy"), pairs)


def swap_core(value):
    return exchange(value, lambda level, band: (level, band ^ 1))


def swap_chip(value):
    bands = lax.axis_size("xy")

    def partner(level, band):
        to = band + 1 if band % 2 else band - 1
        return (level, to) if 0 <= to < bands else (level ^ 2, band)

    return exchange(value, partner)


def swap_pair(value):
    return exchange(value, lambda level, band: (level ^ 1, band))


def swap_far(value, parity):
    levels = lax.axis_size("bins")

    def partner(level, band):
        to = level + 2 if level // 2 % 2 == parity else level - 2
        return (to, band) if 0 <= to < levels else (level, band ^ 1)

    return exchange(value, partner)


def load_kernel(conc, vel_x, vel_y, mask, near, *refs):
    far, (flow, mask_rows, sems) = refs[:-3], refs[-3:]
    _, bins, count, _ = conc.shape
    part = bins // len(far)

    def body(odd):
        near_at, far_at = (0, count - EDGE) if odd else (count - EDGE, 0)
        edges = [(ref, far_at, i * part, part) for i, ref in enumerate(far)] + [(near, near_at, 0, bins)]
        copies = []
        for target, at, low, size in edges:
            for r in range(EDGE):
                copies.append(
                    pltpu.make_async_copy(
                        conc.at[0, pl.ds(low, size), at + r, :], target.at[r, pl.ds(0, size)], sems.at[len(copies)]
                    )
                )
        rows = len(copies)
        for source, target in ((mask, mask_rows), (vel_x.at[0], flow.at[0]), (vel_y.at[0], flow.at[1])):
            copies.append(pltpu.make_async_copy(source, target, sems.at[len(copies)]))
        for copy in copies:
            copy.start()
        for target, _, _, size in edges:
            for r in range(EDGE):
                target[r, size:, :] = jnp.zeros_like(target[r, size:, :])
        for copy in copies[rows:]:
            copy.wait()
        flow[2] = mask_rows[...].astype(jnp.float32)
        for target, at, _, size in edges:
            end = 0 if at == 0 else count - 1
            for i in range(3):
                target[0, size + i : size + i + 1, :] = flow[i, end : end + 1, :]
        for copy in copies[:rows]:
            copy.wait()

    by_parity(body)


def load(conc, vel_x, vel_y, mask):
    _, bins, count, cols = conc.shape
    assert count == 2 * EDGE

    def edge(size):
        return pltpu.VMEM((EDGE, size + SUBLANES, cols), jnp.float32)

    near, *far, flow = pl.pallas_call(
        load_kernel,
        out_shape=(edge(bins), *[edge(bins // PARTS)] * PARTS, pltpu.VMEM((3, count, cols), jnp.float32)),
        in_specs=[HBM] * 4,
        out_specs=(VMEM,) * (2 + PARTS),
        scratch_shapes=[
            pltpu.VMEM((count, cols), jnp.int32),
            pltpu.SemaphoreType.DMA((3 + EDGE * (1 + PARTS),)),
        ],
        compiler_params=PARAMS,
    )(*in_hbm(conc, vel_x, vel_y, mask))
    return near, far, flow


def horizontal_kernel(near, low, near_ref, *refs):
    far_refs, (halo_ref, flow_ref) = refs[: 1 if low is not None else PARTS], refs[1 if low is not None else PARTS :][:2]
    out_ref, scale_ref = refs[-2:]
    _, bins, cols = out_ref.shape
    share = NB // PARTS
    count = flow_ref.shape[1]
    column = lax.broadcasted_iota(jnp.int32, (1, cols), 1)
    block = 16 * SUBLANES

    def body(odd):
        first = odd == near
        order = ("halo", "own", "other") if first else ("other", "own", "halo")
        base = 2 if first else 0

        band = lax.axis_index("xy")
        outside = jnp.logical_and(not near, jnp.logical_or(band == 0, band == lax.axis_size("xy") - 1))
        inside = jnp.where(outside, 0.0, 1.0)
        for i in range(1, 5):
            if order[i // EDGE] == "halo":
                aux = halo_ref[0, bins : bins + SUBLANES, :]
                x, y, water = aux[0:1], aux[1:2], aux[2:3] * inside
            else:
                at = i - base
                x, y, water = (flow_ref[part, at : at + 1, :] for part in range(3))
            x, y = 0.5 * x, 0.5 * y
            east = inside if i == 3 and not first else 1.0
            west = inside if i == 2 and first else 1.0
            parts = (
                water * (1.0 - 4.0 * h_diffusion),
                water * (h_diffusion - x) * east,
                water * (h_diffusion + x) * west,
                jnp.where(column == cols - 1, 0.0, water * (h_diffusion - y)),
                jnp.where(column == 0, 0.0, water * (h_diffusion + y)),
            )
            for number, part in enumerate(parts):
                scale_ref[i - 1, number] = jnp.broadcast_to(part, (SUBLANES, cols))

        def step(cells, i):
            own, east, west, north, south = (
                jnp.concatenate([scale_ref[i - 1, number]] * (block // SUBLANES), 0) for number in range(5)
            )
            here = cells[i]
            return (
                own * here
                + east * cells[i + 1]
                + west * cells[i - 1]
                + north * pltpu.roll(here, cols - 1, 1)
                + south * pltpu.roll(here, 1, 1)
            )

        for at in range(0, bins, block):
            cells = {}
            for i in range(6):
                kind = order[i // EDGE]
                if kind == "halo":
                    ref, place = halo_ref, at
                elif (kind == "own") == near:
                    ref, place = near_ref, at + (low or 0)
                else:
                    ref, place = far_refs[at // share], at % share
                cells[i] = ref[i % EDGE, pl.ds(place, block), :]
            once = {i: step(cells, i) for i in range(1, 5)}
            for i in range(EDGE):
                out_ref[i, pl.ds(at, block), :] = step(once, EDGE + i)

    by_parity(body)


def horizontal(low, near, far, halo, flow, before=()):
    _, bins, cols = halo.shape
    bins -= SUBLANES
    return pl.pallas_call(
        functools.partial(horizontal_kernel, low is None, low),
        out_shape=pltpu.VMEM((EDGE, bins, cols), jnp.float32),
        in_specs=[VMEM] * (3 + len(far)) + [ANY] * len(before),
        out_specs=VMEM,
        scratch_shapes=[pltpu.VMEM((4, 5, SUBLANES, cols), jnp.float32)],
        cost_estimate=pl.CostEstimate(flops=6 * 9 * bins * cols, bytes_accessed=32 * bins * cols, transcendentals=0),
        compiler_params=PARAMS,
    )(*in_vmem(near, *far, halo, flow, *before))


def weigh(table_ref, low, terms):
    out = None
    for column, cells in terms:
        part = cells if column is None else column * cells if not isinstance(column, int) else table_ref[low : low + cells.shape[0], column : column + 1] * cells
        out = part if out is None else out + part
    return out


def combine_kernel(sums, width, table_ref, *refs):
    outs = refs[len(refs) - len(sums) :]
    low = 0
    while low < NB:
        cells, refs = refs[:width], refs[width:]
        size = cells[0].shape[1]
        for r in range(EDGE):
            for terms, out in zip(sums, outs):
                out[r, pl.ds(low, size)] = weigh(table_ref, low, [(at, cells[i][r]) for i, at in enumerate(terms)])
        low += size


def combine(table, parts, sums, before=()):
    cells = [value for part in parts for value in part]
    shape = (EDGE, NB, cells[0].shape[2])
    outs = pl.pallas_call(
        functools.partial(combine_kernel, sums, len(parts[0])),
        out_shape=(pltpu.VMEM(shape, jnp.float32),) * len(sums),
        in_specs=[VMEM] * (1 + len(cells)) + [ANY] * len(before),
        out_specs=(VMEM,) * len(sums),
        cost_estimate=pl.CostEstimate(
            flops=6 * NB * EDGE * shape[2], bytes_accessed=20 * NB * EDGE * shape[2], transcendentals=0
        ),
        compiler_params=PARAMS,
    )(*in_vmem(table, *cells, *before))
    return list(outs)


def split(value):
    high = value.astype(jnp.bfloat16)
    return high, (value - high.astype(jnp.float32)).astype(jnp.bfloat16)


def collide_kernel(chunks, table_ref, both_ref, *refs):
    out_ref, done_ref, sems = refs[-3:]
    count, cols = out_ref.shape[2:]

    levels, k = lax.axis_size("bins"), lax.axis_index("bins")
    below, above = jnp.where(k >= 2, 1.0, 0.0), jnp.where(k + 2 < levels, 1.0, 0.0)
    high_z = (k // 2) % 2 == 1
    there = {"there_0": jnp.where(high_z, below, above), "there_1": jnp.where(high_z, above, below)}

    def body(odd):
        copies, first = [], 0
        for near, parts in chunks:
            at = 0 if odd == near else count - EDGE
            rows = [[] for _ in range(EDGE)]
            for low, columns in parts:
                cells = refs[first : first + len(columns)]
                first += len(columns)
                for r in range(EDGE):
                    rows[r].append(
                        weigh(table_ref, low, [(there.get(column, column), ref[r]) for column, ref in zip(columns, cells)])
                    )
            cells = jnp.concatenate([jnp.concatenate(pieces, 0) for pieces in rows], 1)
            high, low = split(cells)
            sums = jnp.dot(both_ref[...], jnp.concatenate([high, low, high], 0), preferred_element_type=jnp.float32)
            result = cells + cells * sums[:NB] + sums[NB:]
            for r in range(EDGE):
                slot = len(copies)
                done_ref[slot] = result[:, r * cols : (r + 1) * cols]
                copies.append(pltpu.make_async_copy(done_ref.at[slot], out_ref.at[0, :, at + r, :], sems.at[slot]))
                copies[-1].start()
        for copy in copies:
            copy.wait()

    by_parity(body)


def collide(table, both, chunks, shape, before=None):
    rest = () if before is None else (before,)
    cells = [value for _, parts in chunks for _, terms in parts for _, value in terms]
    chunks = [(near, [(low, [column for column, _ in terms]) for low, terms in parts]) for near, parts in chunks]
    rows, cols = EDGE * len(chunks), shape[3]
    return pl.pallas_call(
        functools.partial(collide_kernel, chunks),
        out_shape=pltpu.HBM(shape, jnp.float32),
        in_specs=[VMEM] * (2 + len(cells)) + [HBM] * len(rest),
        out_specs=HBM,
        input_output_aliases={2 + len(cells): 0} if rest else {},
        scratch_shapes=[pltpu.VMEM((rows, NB, cols), jnp.float32), pltpu.SemaphoreType.DMA((rows,))],
        cost_estimate=pl.CostEstimate(
            flops=12 * NB * NB * rows * cols, bytes_accessed=24 * rows * NB * cols, transcendentals=0
        ),
        compiler_params=PARAMS,
    )(*in_vmem(table, both, *cells), *in_hbm(*rest))


def local(
    conc,
    vel_x,
    vel_y,
    sea_mask,
    settle,
    size_bin_kernel_class,
    aggregate_upward_factor,
    agg_down,
    break_rate,
):
    near_edge, far_edges, flow = load(conc, vel_x, vel_y, sea_mask)
    halo_chip = [swap_chip(edge) for edge in far_edges]
    halo_core = swap_core(near_edge)
    near = horizontal(None, near_edge, far_edges, halo_core, flow)
    part = NB // PARTS
    far, before = [], (near,)
    for i, edge in enumerate(far_edges):
        far.append(horizontal(i * part, near_edge, [edge], halo_chip[i], flow, before))
        before = (far[-1],)

    levels = lax.axis_size("bins")
    k = lax.axis_index("bins")
    odd = k % 2 == 1
    high_z = (k // 2) % 2 == 1
    fall = settle + v_diffusion
    rise = jnp.full_like(settle, v_diffusion)

    def keep(level):
        inner = (level > 0).astype(jnp.float32) + (level < levels - 1).astype(jnp.float32)
        return 1.0 - settle - v_diffusion * inner

    inner = (k > 0).astype(jnp.float32) + (k < levels - 1).astype(jnp.float32)
    on_self = keep(k) * keep(k) + inner * fall * rise
    up2, down2 = fall * fall, rise * rise
    zero = jnp.zeros_like(settle)
    up_pair = jnp.where(odd, zero, fall * (keep(k + 2) + keep(k + 1)))
    down_pair = jnp.where(odd, rise * (keep(k - 2) + keep(k - 1)), zero)
    send_0 = (jnp.where(high_z, down2, up2), jnp.where(high_z, down_pair, up_pair))
    send_1 = (jnp.where(high_z, up2, down2), jnp.where(high_z, up_pair, down_pair))
    from_pair = jnp.where(odd, fall * (keep(k) + keep(k - 1)), rise * (keep(k) + keep(k + 1)))
    pair_own = jnp.where(odd, rise * (keep(k - 1) + keep(k)), fall * (keep(k + 1) + keep(k)))
    pair_far = jnp.where(odd, fall * (keep(k - 1) + keep(k - 2)), rise * (keep(k + 1) + keep(k + 2)))
    below, above = (k >= 2).astype(jnp.float32), (k + 2 < levels).astype(jnp.float32)
    there_0, there_1 = jnp.where(high_z, below, above), jnp.where(high_z, above, below)
    from_0 = jnp.where(high_z, up2, down2) * there_0
    from_1 = jnp.where(high_z, down2, up2) * there_1
    pair_far = pair_far * jnp.where(odd, below, above)
    uses_0 = odd == high_z

    onehot = (size_bin_kernel_class[:, None] == jnp.arange(NCLS)[None, :]).astype(jnp.float32)

    def lookup(table):
        return jnp.sum(onehot * table[None, :], 1)

    up_rate = lookup(aggregate_upward_factor)
    down_rate = lookup(agg_down)
    brk_rate = lookup(break_rate)
    index = jnp.arange(NB)
    i, j = index[None, :], index[:, None]
    weight = 1.0 / jnp.maximum(index, 1).astype(jnp.float32)
    matrix = jnp.where(i < j, down_rate[:, None] * up_rate[None, :], 0.0) - jnp.where(
        i > j, up_rate[:, None] * down_rate[None, :], 0.0
    )
    pieces = jnp.where(i > j, (brk_rate * weight)[None, :], 0.0) - jnp.where(
        (i == j) & (j >= 1), brk_rate[:, None], 0.0
    )
    both = jnp.concatenate([matrix * (step_duration * collide_scale / NB), pieces * step_duration], 0)

    high = lax.reduce_precision(both, 8, 7)
    low = both - high
    both = jnp.concatenate([high, high, low], 1).astype(jnp.bfloat16)

    columns = [
        send_0[0], send_0[1], send_1[0], send_1[1], on_self, from_pair, there_0 + zero, there_1 + zero,
        pair_own, jnp.where(uses_0, pair_far, zero), jnp.where(uses_0, zero, pair_far), from_0, from_1, zero + 1.0,
    ]
    table = jnp.pad(jnp.stack(columns, 1), ((0, 0), (0, 128 - len(columns))))

    far_1 = swap_far(near, 1)
    far_0 = swap_far(near, 0)
    pairs_far = [(cells, swap_pair(cells)) for cells in far]
    (send,) = combine(table, [(near, far_0, far_1)], ((8, 9, 10),))
    pair = swap_pair(send)
    sends = combine(table, pairs_far, ((0, 1),), (send,))
    sends += combine(table, pairs_far, ((2, 3), (4, 5)), (sends[0],))
    back_1 = swap_far(sends[1], 1)
    back_0 = swap_far(sends[0], 0)
    half = collide(table, both, [(True, [(0, [(4, near), (11, far_0), (12, far_1), (None, pair)])])], conc.shape)
    return collide(table, both, [(False, [(0, [(None, sends[2]), ("there_0", back_0), ("there_1", back_1)])])], conc.shape, half)


def solution(mesh):
    placed = (
        P("bins", None, "xy", None),
        P("bins", "xy", None),
        P("bins", "xy", None),
        P("xy", None),
        P(),
        P(),
        P(),
        P(),
        P(),
    )
    return jax.shard_map(
        local, mesh=mesh, in_specs=placed, out_specs=P("bins", None, "xy", None), check_vma=False
    )
```

```python
import functools

import jax
import jax.numpy as jnp
from jax import lax
from jax.experimental import pallas as pl
from jax.experimental.pallas import tpu as pltpu
from jax.sharding import PartitionSpec as P

NB = 128
NCLS = 8

h_diffusion = 0.2
v_diffusion = 0.2
step_duration = 0.5
collide_scale = 2.0
SUBLANES = 8
EDGE = 2
PARTS = 1
VMEM = pl.BlockSpec(memory_space=pltpu.VMEM)
HBM = pl.BlockSpec(memory_space=pltpu.HBM)
ANY = pl.BlockSpec(memory_space=pl.ANY)
PARAMS = pltpu.CompilerParams(vmem_limit_bytes=8 << 20)


def in_vmem(*values):
    return [pltpu.with_memory_space_constraint(value, pltpu.VMEM) for value in values]


def in_hbm(*values):
    return [pltpu.with_memory_space_constraint(value, pltpu.HBM) for value in values]


def odd_core():
    return lax.axis_index("xy") % 2 == 1


def by_parity(body):
    odd = odd_core()
    pl.when(odd)(functools.partial(body, True))
    pl.when(jnp.logical_not(odd))(functools.partial(body, False))


def exchange(value, partner):
    bands = lax.axis_size("xy")
    pairs = []
    for level in range(lax.axis_size("bins")):
        for band in range(bands):
            to_level, to_band = partner(level, band)
            pairs.append((level * bands + band, to_level * bands + to_band))
    return lax.ppermute(value, ("bins", "xy"), pairs)


def swap_core(value):
    return exchange(value, lambda level, band: (level, band ^ 1))


def swap_chip(value):
    bands = lax.axis_size("xy")

    def partner(level, band):
        to = band + 1 if band % 2 else band - 1
        return (level, to) if 0 <= to < bands else (level ^ 2, band)

    return exchange(value, partner)


def swap_pair(value):
    return exchange(value, lambda level, band: (level ^ 1, band))


def swap_far(value, parity):
    levels = lax.axis_size("bins")

    def partner(level, band):
        to = level + 2 if level // 2 % 2 == parity else level - 2
        return (to, band) if 0 <= to < levels else (level, band ^ 1)

    return exchange(value, partner)


def load_kernel(conc, vel_x, vel_y, mask, near, *refs):
    far, (flow, mask_rows, sems) = refs[:-3], refs[-3:]
    _, bins, count, _ = conc.shape
    part = bins // len(far)

    def body(odd):
        near_at, far_at = (0, count - EDGE) if odd else (count - EDGE, 0)
        edges = [(ref, far_at, i * part, part) for i, ref in enumerate(far)] + [(near, near_at, 0, bins)]
        copies = []
        for target, at, low, size in edges:
            for r in range(EDGE):
                copies.append(
                    pltpu.make_async_copy(
                        conc.at[0, pl.ds(low, size), at + r, :], target.at[r, pl.ds(0, size)], sems.at[len(copies)]
                    )
                )
        rows = len(copies)
        for source, target in ((mask, mask_rows), (vel_x.at[0], flow.at[0]), (vel_y.at[0], flow.at[1])):
            copies.append(pltpu.make_async_copy(source, target, sems.at[len(copies)]))
        for copy in copies:
            copy.start()
        for target, _, _, size in edges:
            target[1, size:, :] = jnp.zeros_like(target[1, size:, :])
        for copy in copies[rows:]:
            copy.wait()
        flow[2] = mask_rows[...].astype(jnp.float32)
        for target, at, _, size in edges:
            end = 0 if at == 0 else count - 1
            ends = [flow[i, end : end + 1, :] for i in range(3)]
            target[0, size:, :] = jnp.concatenate(ends + [jnp.zeros((SUBLANES - 3, ends[0].shape[1]), jnp.float32)], 0)
        for copy in copies[:rows]:
            copy.wait()

    by_parity(body)


def load(conc, vel_x, vel_y, mask):
    _, bins, count, cols = conc.shape
    assert count == 2 * EDGE

    def edge(size):
        return pltpu.VMEM((EDGE, size + SUBLANES, cols), jnp.float32)

    near, *far, flow = pl.pallas_call(
        load_kernel,
        out_shape=(edge(bins), *[edge(bins // PARTS)] * PARTS, pltpu.VMEM((3, count, cols), jnp.float32)),
        in_specs=[HBM] * 4,
        out_specs=(VMEM,) * (2 + PARTS),
        scratch_shapes=[
            pltpu.VMEM((count, cols), jnp.int32),
            pltpu.SemaphoreType.DMA((3 + EDGE * (1 + PARTS),)),
        ],
        compiler_params=PARAMS,
    )(*in_hbm(conc, vel_x, vel_y, mask))
    return near, far, flow


def horizontal_kernel(near, low, near_ref, *refs):
    far_refs, (halo_ref, flow_ref) = refs[: 1 if low is not None else PARTS], refs[1 if low is not None else PARTS :][:2]
    out_ref, scale_ref = refs[-2:]
    _, bins, cols = out_ref.shape
    share = NB // PARTS
    count = flow_ref.shape[1]
    column = lax.broadcasted_iota(jnp.int32, (1, cols), 1)
    block = 16 * SUBLANES

    def body(odd):
        first = odd == near
        order = ("halo", "own", "other") if first else ("other", "own", "halo")
        base = 2 if first else 0

        band = lax.axis_index("xy")
        outside = jnp.logical_and(not near, jnp.logical_or(band == 0, band == lax.axis_size("xy") - 1))
        inside = jnp.where(outside, 0.0, 1.0)
        for i in range(1, 5):
            if order[i // EDGE] == "halo":
                aux = halo_ref[0, bins : bins + SUBLANES, :]
                x, y, water = aux[0:1], aux[1:2], aux[2:3] * inside
            else:
                at = i - base
                x, y, water = (flow_ref[part, at : at + 1, :] for part in range(3))
            x, y = 0.5 * x, 0.5 * y
            east = inside if i == 3 and not first else 1.0
            west = inside if i == 2 and first else 1.0
            parts = (
                water * (1.0 - 4.0 * h_diffusion),
                water * (h_diffusion - x) * east,
                water * (h_diffusion + x) * west,
                jnp.where(column == cols - 1, 0.0, water * (h_diffusion - y)),
                jnp.where(column == 0, 0.0, water * (h_diffusion + y)),
            )
            for number, part in enumerate(parts):
                scale_ref[i - 1, number] = jnp.broadcast_to(part, (SUBLANES, cols))

        def step(cells, i):
            own, east, west, north, south = (
                jnp.concatenate([scale_ref[i - 1, number]] * (block // SUBLANES), 0) for number in range(5)
            )
            here = cells[i]
            return (
                own * here
                + east * cells[i + 1]
                + west * cells[i - 1]
                + north * pltpu.roll(here, cols - 1, 1)
                + south * pltpu.roll(here, 1, 1)
            )

        for at in range(0, bins, block):
            cells = {}
            for i in range(6):
                kind = order[i // EDGE]
                if kind == "halo":
                    ref, place = halo_ref, at
                elif (kind == "own") == near:
                    ref, place = near_ref, at + (low or 0)
                else:
                    ref, place = far_refs[at // share], at % share
                cells[i] = ref[i % EDGE, pl.ds(place, block), :]
            once = {i: step(cells, i) for i in range(1, 5)}
            for i in range(EDGE):
                out_ref[i, pl.ds(at, block), :] = step(once, EDGE + i)

    by_parity(body)


def horizontal(low, near, far, halo, flow, before=()):
    _, bins, cols = halo.shape
    bins -= SUBLANES
    return pl.pallas_call(
        functools.partial(horizontal_kernel, low is None, low),
        out_shape=pltpu.VMEM((EDGE, bins, cols), jnp.float32),
        in_specs=[VMEM] * (3 + len(far)) + [ANY] * len(before),
        out_specs=VMEM,
        scratch_shapes=[pltpu.VMEM((4, 5, SUBLANES, cols), jnp.float32)],
        cost_estimate=pl.CostEstimate(flops=6 * 9 * bins * cols, bytes_accessed=32 * bins * cols, transcendentals=0),
        compiler_params=PARAMS,
    )(*in_vmem(near, *far, halo, flow, *before))


def weigh(table_ref, low, terms):
    out = None
    for column, cells in terms:
        part = cells if column is None else column * cells if not isinstance(column, int) else table_ref[low : low + cells.shape[0], column : column + 1] * cells
        out = part if out is None else out + part
    return out


def combine_kernel(sums, width, table_ref, *refs):
    outs = refs[len(refs) - len(sums) :]
    low = 0
    while low < NB:
        cells, refs = refs[:width], refs[width:]
        size = cells[0].shape[1]
        for r in range(EDGE):
            for terms, out in zip(sums, outs):
                out[r, pl.ds(low, size)] = weigh(table_ref, low, [(at, cells[i][r]) for i, at in enumerate(terms)])
        low += size


def combine(table, parts, sums, before=()):
    cells = [value for part in parts for value in part]
    shape = (EDGE, NB, cells[0].shape[2])
    outs = pl.pallas_call(
        functools.partial(combine_kernel, sums, len(parts[0])),
        out_shape=(pltpu.VMEM(shape, jnp.float32),) * len(sums),
        in_specs=[VMEM] * (1 + len(cells)) + [ANY] * len(before),
        out_specs=(VMEM,) * len(sums),
        cost_estimate=pl.CostEstimate(
            flops=6 * NB * EDGE * shape[2], bytes_accessed=20 * NB * EDGE * shape[2], transcendentals=0
        ),
        compiler_params=PARAMS,
    )(*in_vmem(table, *cells, *before))
    return list(outs)


def split(value):
    high = value.astype(jnp.bfloat16)
    return high, (value - high.astype(jnp.float32)).astype(jnp.bfloat16)


def collide_kernel(chunks, table_ref, both_ref, *refs):
    out_ref, done_ref, sems = refs[-3:]
    count, cols = out_ref.shape[2:]

    levels, k = lax.axis_size("bins"), lax.axis_index("bins")
    below, above = jnp.where(k >= 2, 1.0, 0.0), jnp.where(k + 2 < levels, 1.0, 0.0)
    high_z = (k // 2) % 2 == 1
    there = {"there_0": jnp.where(high_z, below, above), "there_1": jnp.where(high_z, above, below)}

    def body(odd):
        copies, first = [], 0
        for near, parts in chunks:
            at = 0 if odd == near else count - EDGE
            rows = [[] for _ in range(EDGE)]
            for low, columns in parts:
                cells = refs[first : first + len(columns)]
                first += len(columns)
                for r in range(EDGE):
                    rows[r].append(
                        weigh(table_ref, low, [(there.get(column, column), ref[r]) for column, ref in zip(columns, cells)])
                    )
            cells = jnp.concatenate([jnp.concatenate(pieces, 0) for pieces in rows], 1)
            high, low = split(cells)
            sums = jnp.dot(both_ref[...], jnp.concatenate([high, low, high], 0), preferred_element_type=jnp.float32)
            result = cells + cells * sums[:NB] + sums[NB:]
            for r in range(EDGE):
                slot = len(copies)
                done_ref[slot] = result[:, r * cols : (r + 1) * cols]
                copies.append(pltpu.make_async_copy(done_ref.at[slot], out_ref.at[0, :, at + r, :], sems.at[slot]))
                copies[-1].start()
        for copy in copies:
            copy.wait()

    by_parity(body)


def collide(table, both, chunks, shape, before=None):
    rest = () if before is None else (before,)
    cells = [value for _, parts in chunks for _, terms in parts for _, value in terms]
    chunks = [(near, [(low, [column for column, _ in terms]) for low, terms in parts]) for near, parts in chunks]
    rows, cols = EDGE * len(chunks), shape[3]
    return pl.pallas_call(
        functools.partial(collide_kernel, chunks),
        out_shape=pltpu.HBM(shape, jnp.float32),
        in_specs=[VMEM] * (2 + len(cells)) + [HBM] * len(rest),
        out_specs=HBM,
        input_output_aliases={2 + len(cells): 0} if rest else {},
        scratch_shapes=[pltpu.VMEM((rows, NB, cols), jnp.float32), pltpu.SemaphoreType.DMA((rows,))],
        cost_estimate=pl.CostEstimate(
            flops=12 * NB * NB * rows * cols, bytes_accessed=24 * rows * NB * cols, transcendentals=0
        ),
        compiler_params=PARAMS,
    )(*in_vmem(table, both, *cells), *in_hbm(*rest))


def local(
    conc,
    vel_x,
    vel_y,
    sea_mask,
    settle,
    size_bin_kernel_class,
    aggregate_upward_factor,
    agg_down,
    break_rate,
):
    near_edge, far_edges, flow = load(conc, vel_x, vel_y, sea_mask)
    halo_chip = [swap_chip(edge) for edge in far_edges]
    halo_core = swap_core(near_edge)
    near = horizontal(None, near_edge, far_edges, halo_core, flow)
    part = NB // PARTS
    far, before = [], (near,)
    for i, edge in enumerate(far_edges):
        far.append(horizontal(i * part, near_edge, [edge], halo_chip[i], flow, before))
        before = (far[-1],)

    levels = lax.axis_size("bins")
    k = lax.axis_index("bins")
    odd = k % 2 == 1
    high_z = (k // 2) % 2 == 1
    fall = settle + v_diffusion
    rise = jnp.full_like(settle, v_diffusion)

    def keep(level):
        inner = (level > 0).astype(jnp.float32) + (level < levels - 1).astype(jnp.float32)
        return 1.0 - settle - v_diffusion * inner

    inner = (k > 0).astype(jnp.float32) + (k < levels - 1).astype(jnp.float32)
    on_self = keep(k) * keep(k) + inner * fall * rise
    up2, down2 = fall * fall, rise * rise
    zero = jnp.zeros_like(settle)
    up_pair = jnp.where(odd, zero, fall * (keep(k + 2) + keep(k + 1)))
    down_pair = jnp.where(odd, rise * (keep(k - 2) + keep(k - 1)), zero)
    send_0 = (jnp.where(high_z, down2, up2), jnp.where(high_z, down_pair, up_pair))
    send_1 = (jnp.where(high_z, up2, down2), jnp.where(high_z, up_pair, down_pair))
    from_pair = jnp.where(odd, fall * (keep(k) + keep(k - 1)), rise * (keep(k) + keep(k + 1)))
    pair_own = jnp.where(odd, rise * (keep(k - 1) + keep(k)), fall * (keep(k + 1) + keep(k)))
    pair_far = jnp.where(odd, fall * (keep(k - 1) + keep(k - 2)), rise * (keep(k + 1) + keep(k + 2)))
    below, above = (k >= 2).astype(jnp.float32), (k + 2 < levels).astype(jnp.float32)
    there_0, there_1 = jnp.where(high_z, below, above), jnp.where(high_z, above, below)
    from_0 = jnp.where(high_z, up2, down2) * there_0
    from_1 = jnp.where(high_z, down2, up2) * there_1
    pair_far = pair_far * jnp.where(odd, below, above)
    uses_0 = odd == high_z

    onehot = (size_bin_kernel_class[:, None] == jnp.arange(NCLS)[None, :]).astype(jnp.float32)

    def lookup(table):
        return jnp.sum(onehot * table[None, :], 1)

    up_rate = lookup(aggregate_upward_factor)
    down_rate = lookup(agg_down)
    brk_rate = lookup(break_rate)
    index = jnp.arange(NB)
    i, j = index[None, :], index[:, None]
    weight = 1.0 / jnp.maximum(index, 1).astype(jnp.float32)
    matrix = jnp.where(i < j, down_rate[:, None] * up_rate[None, :], 0.0) - jnp.where(
        i > j, up_rate[:, None] * down_rate[None, :], 0.0
    )
    pieces = jnp.where(i > j, (brk_rate * weight)[None, :], 0.0) - jnp.where(
        (i == j) & (j >= 1), brk_rate[:, None], 0.0
    )
    both = jnp.concatenate([matrix * (step_duration * collide_scale / NB), pieces * step_duration], 0)

    high = lax.reduce_precision(both, 8, 7)
    low = both - high
    both = jnp.concatenate([high, high, low], 1).astype(jnp.bfloat16)

    columns = [
        send_0[0], send_0[1], send_1[0], send_1[1], on_self, from_pair, there_0 + zero, there_1 + zero,
        pair_own, jnp.where(uses_0, pair_far, zero), jnp.where(uses_0, zero, pair_far), from_0, from_1, zero + 1.0,
    ]
    table = jnp.pad(jnp.stack(columns, 1), ((0, 0), (0, 128 - len(columns))))

    far_1 = swap_far(near, 1)
    far_0 = swap_far(near, 0)
    pairs_far = [(cells, swap_pair(cells)) for cells in far]
    (send,) = combine(table, [(near, far_0, far_1)], ((8, 9, 10),))
    pair = swap_pair(send)
    sends = combine(table, pairs_far, ((0, 1),), (send,))
    sends += combine(table, pairs_far, ((2, 3), (4, 5)), (sends[0],))
    back_1 = swap_far(sends[1], 1)
    back_0 = swap_far(sends[0], 0)
    half = collide(table, both, [(True, [(0, [(4, near), (11, far_0), (12, far_1), (None, pair)])])], conc.shape)
    return collide(table, both, [(False, [(0, [(None, sends[2]), ("there_0", back_0), ("there_1", back_1)])])], conc.shape, half)


def solution(mesh):
    placed = (
        P("bins", None, "xy", None),
        P("bins", "xy", None),
        P("bins", "xy", None),
        P("xy", None),
        P(),
        P(),
        P(),
        P(),
        P(),
    )
    return jax.shard_map(
        local, mesh=mesh, in_specs=placed, out_specs=P("bins", None, "xy", None), check_vma=False
    )
```
